128 devices in a mesh: grp: 32 (over x, z, core), blk: 4 (over y).
Axes of the slice: x: 4, y: 4, z: 4, core: 2. Of those that a mesh axis runs over, the one named last changes fastest.
Arguments:
- embeddings: bfloat16 [131072, 1024], P(('grp', 'blk')), may hold values from -6 to 6
- labels: int32 [131072, 1], P(('grp', 'blk')), may hold values from 0 to 127; in each aligned block of 1024 rows (0 to 1023, 1024 to 2047, ...) at most 12 rows name the same one
- order_ids: int32 [131072], P(('grp', 'blk')), may hold values from 0 to 131071, each once
Outputs:
- best_match: float32 [131072], P(('grp', 'blk'))
The draws below stay inside these ranges and needn't reach their ends.
Inputs may be any that keep to these rules, and one draw needn't show every extreme that they name: `labels`: among the 1024 documents of one device, no cluster holds more than 12; some cluster holds exactly 12 in some devices' rows. Every cluster has some document. `order_ids`: every place 0 to 131071 once.
All inputs are finite; a program needn't handle non-finite values.
Results may differ from the reference program's by a relative error of at most 0.0014.
Values may be sent and summed in bfloat16 or wider, within the bound.
No kernel may reach another device: no remote copies, remote signals or barrier semaphores. Data moves between devices by JAX's collectives and lax.ppermute only.
A program may use at most 64 MiB of HBM per device.

```python
import math
import jax
import jax.numpy as jnp
import numpy as np
from jax import lax

D = 1024
ROWS = 1024
CLUSTERS = 128
CAP = 12
TOTAL = 131072


def levels(stream_key, dims, split, low, largest):
    def one(dim, blocks):
        draws = jax.random.uniform(jax.random.fold_in(jax.random.fold_in(stream_key, 6), dim), (blocks,), jnp.float32, low / len(split), largest / len(split))
        return jnp.repeat(jnp.exp(draws), dims[dim] // blocks).reshape((-1,) + (1,) * (len(dims) - dim - 1))

    level = one(*split[0])
    for cut in split[1:]:
        level = level * one(*cut)
    return level


def assign_block(key, own, number, rows, number_of, top, limit, slope):
    order = jax.random.permutation(key, number_of)
    packed, usual = portions_of(number_of, rows * top, limit, slope, True), portions_of(number_of, rows * top, limit, slope, False)
    places = jnp.arange(number_of)

    def named(tallies, offset_by):
        used = int((tallies > 0).sum())
        fixed = max(1, used // 4)
        moved = fixed + (places - fixed + offset_by * (used - fixed)) % max(1, number_of - fixed)
        return jnp.zeros((number_of,), jnp.int32).at[order[jnp.where(places < fixed, places, moved)]].set(jnp.asarray(tallies, jnp.int32))

    tallies = jnp.where(number % 4 == 0, named(packed, number // 4), named(usual, number - number // 4 - 1))
    mixed = jax.random.permutation(jax.random.fold_in(own, 3), number_of)
    giver, sink = mixed[0:number_of // 2 * 2:2], mixed[1:number_of // 2 * 2:2]
    slack = jnp.minimum(tallies[giver] - 1, limit - tallies[sink]) // 2
    slack = jnp.where((giver == order[0]) | (sink == order[0]) | (tallies[sink] == 0), 0, jnp.maximum(slack, 0))
    moved = jax.random.randint(jax.random.fold_in(own, 4), (number_of // 2,), 0, 1 << 20) % (slack + 1)
    tallies = tallies.at[giver].add(-moved).at[sink].add(moved)
    items = jnp.searchsorted(jnp.cumsum(tallies), jnp.arange(rows * top), side="right").astype(jnp.int32)
    table = items.reshape(top, rows).T
    table = table[jax.random.permutation(jax.random.fold_in(own, 1), rows)]
    offset_by = jax.random.randint(jax.random.fold_in(own, 2), (rows, 1), 0, top)
    return jnp.take_along_axis(table, (jnp.arange(top)[None, :] + offset_by) % top, axis=1)


def portions_of(amount, total, reach, lean, full):
    weights = [(1 << 20) // math.isqrt(standing ** lean) + 1 for standing in range(1, amount + 1)]
    largest = reach if full else min(reach, max(-(-total // amount), total * weights[0] // sum(weights)))
    least = 1 if total - largest >= amount - 1 else 0
    holding, spare = [largest] + [least] * (amount - 1), total - largest - least * (amount - 1)
    while spare > 0:
        candidates = [i for i in range(1, amount) if holding[i] < largest] or [i for i in range(1, amount) if holding[i] < reach]
        pool, budget = sum([weights[i] for i in candidates]), spare
        for i in candidates:
            extra = min(reach - holding[i], max(1, budget * weights[i] // pool), spare)
            holding[i] = holding[i] + extra
            spare = spare - extra
    return np.array(holding)


def noise(own_key, shape, scale, limit, split=(), kind=jnp.bfloat16):
    values = scale * jax.random.normal(own_key, shape, jnp.float32)
    if split:
        values = values * levels(own_key, shape, split, -0.22, 0.18)
    return jnp.clip(values, -limit, limit).astype(kind)


def setup_inputs(seed: int = 0) -> dict:
    key_of = jax.random.split(jax.random.key(seed), 4)
    embeddings = noise(key_of[0], (TOTAL, D), 1.0, 6.0, ((0, 128),))
    labels_keys = jax.random.split(jax.random.fold_in(key_of[1], 1), TOTAL // ROWS)
    labels_turns = jax.random.permutation(jax.random.fold_in(key_of[1], 3), TOTAL // ROWS)
    labels = jax.vmap(lambda own, number: assign_block(jax.random.fold_in(key_of[1], 2), own, number, ROWS, CLUSTERS, 1, CAP, 2))(labels_keys, labels_turns).reshape((TOTAL, 1))
    order_ids = jax.random.permutation(key_of[2], TOTAL).astype(jnp.int32)
    return dict(embeddings=embeddings, labels=labels, order_ids=order_ids)


far_order = 1 << 30

def reference(embeddings, labels, order_ids):
    values = embeddings.astype(jnp.float32)
    scale = lax.rsqrt(lax.optimization_barrier(jnp.mean(values * values, axis=1, keepdims=True)) + 1e-06) * D ** (-0.5)
    unit = (values * scale).astype(jnp.bfloat16)
    label_flat = labels[:, 0].astype(jnp.int32)
    blocks = label_flat.reshape(CLUSTERS, ROWS)
    onehot = (blocks[:, :, None] == jnp.arange(CLUSTERS, dtype=jnp.int32)[None, None, :]).astype(jnp.int32)
    position = (lax.optimization_barrier(jnp.sum(jnp.cumsum(onehot, axis=1) * onehot, axis=2)) - 1).reshape(TOTAL)
    source = (jnp.arange(TOTAL, dtype=jnp.int32) // ROWS).astype(jnp.int32)
    width = CLUSTERS * CAP
    slots = ((label_flat * CLUSTERS + source) * CAP + position).astype(jnp.int32)
    keys = jnp.zeros((CLUSTERS * width, D), jnp.bfloat16).at[slots].set(unit).reshape(CLUSTERS, width, D)
    orders = jnp.full((CLUSTERS * width,), far_order, jnp.int32).at[slots].set(order_ids.astype(jnp.int32)).reshape(CLUSTERS, width)

    def per_cluster(pair):
        members, places = pair
        scores = jnp.dot(members, members.T, preferred_element_type=jnp.float32)
        earlier = places[None, :] < places[:, None]
        return lax.optimization_barrier(jnp.max(jnp.where(earlier, scores, jnp.float32(-1.0)), axis=1))
    maxima = lax.map(per_cluster, (keys, orders))
    return maxima.reshape(-1)[slots]
```

```python
import jax
import jax.numpy as jnp
from jax import lax
from jax.experimental import pallas as pl
from jax.experimental.pallas import tpu as pltpu
from jax.sharding import PartitionSpec as P

MAIN = 8
TAIL = 4
NT = (((1,), (1,)), ((), ()))
VMEM_LIMIT = 48 * 1024 * 1024


def fold_pair(low, high, upper):
    first = jnp.where(upper, pltpu.roll(high, 4, 0), low)
    second = jnp.where(upper, high, pltpu.roll(low, 4, 0))
    return first, second


def place_kernel(rows_ref, label_ref, order_ref, out_ref, position_ref, unit, digits, slots):
    step = pl.program_id(0)
    count, width = rows_ref.shape
    partners = out_ref.shape[0]
    devices = partners * pl.num_programs(0)

    @pl.when(step == 0)
    def _():
        labels = label_ref[...]
        carry = jnp.zeros((devices, 128), jnp.float32)
        inner = lax.broadcasted_iota(jnp.int32, (128, 256), 0)
        outer = lax.broadcasted_iota(jnp.int32, (128, 256), 1)
        before = ((inner < outer) | (outer >= 128)).astype(jnp.bfloat16)
        for block in range(count // 128):
            part = labels[:, block * 128 : (block + 1) * 128]
            member = lax.broadcasted_iota(jnp.int32, (devices, 128), 0) == part
            sums = jnp.dot(
                member.astype(jnp.bfloat16), before, preferred_element_type=jnp.float32
            )
            rank = jnp.where(member, sums[:, :128] + carry, 0.0)
            carry = carry + sums[:, 128:]
            position = jnp.sum(rank, axis=0, keepdims=True).astype(jnp.int32)
            position_ref[:, block * 128 : (block + 1) * 128] = position
            slots[0:1, block * 128 : (block + 1) * 128] = jnp.where(
                position < MAIN, part * MAIN + position, -1
            )
            slots[1:2, block * 128 : (block + 1) * 128] = jnp.where(
                position < MAIN, -1, part * TAIL + position - MAIN
            )
        order = order_ref[...]
        line = lax.broadcasted_iota(jnp.int32, (128, count), 0)
        digit = jnp.where(
            (line == 0) | (line == 4),
            order >> 12,
            jnp.where(
                (line == 1) | (line == 5),
                (order >> 6) & 63,
                jnp.where(
                    (line == 2) | (line == 6),
                    order & 63,
                    jnp.where((line == 3) | (line == 7), 1, 0),
                ),
            ),
        )
        digits[...] = digit.astype(jnp.float32).astype(jnp.bfloat16)
        for block in range(count // 128):
            values = rows_ref[block * 128 : (block + 1) * 128, :].astype(jnp.float32)
            scale = lax.rsqrt(
                jnp.mean(values * values, axis=1, keepdims=True) + 1e-06
            ) * width ** (-0.5)
            unit[block * 128 : (block + 1) * 128, :] = (values * scale).astype(jnp.bfloat16)

    slot = slots[...]
    main_rows, tail_rows = partners * MAIN, partners * TAIL
    main_at = lax.broadcasted_iota(jnp.int32, (main_rows, count), 0) + step * main_rows
    tail_at = lax.broadcasted_iota(jnp.int32, (tail_rows, count), 0) + step * tail_rows
    main_pick = (main_at == slot[0:1]).astype(jnp.bfloat16)
    tail_pick = (tail_at == slot[1:2]).astype(jnp.bfloat16)
    main = jnp.dot(main_pick, unit[...], preferred_element_type=jnp.float32)
    tail = jnp.dot(tail_pick, unit[...], preferred_element_type=jnp.float32)
    main_digits = lax.dot_general(
        main_pick, digits[...], NT, preferred_element_type=jnp.float32
    )
    tail_digits = lax.dot_general(
        tail_pick, digits[...], NT, preferred_element_type=jnp.float32
    )
    half = width // 2
    upper_half = lax.broadcasted_iota(jnp.int32, (8, half), 0) >= 4
    upper_line = lax.broadcasted_iota(jnp.int32, (8, 128), 0) >= 4
    left = lax.broadcasted_iota(jnp.int32, (8, 128), 1) < 4
    for partner in range(partners):
        out_ref[partner, :, :width] = main[partner * 8 : (partner + 1) * 8, :].astype(
            jnp.bfloat16
        )
    for pair in range(partners // 2):
        rows = tail[pair * 8 : (pair + 1) * 8, :]
        first, second = fold_pair(rows[:, :half], rows[:, half:], upper_half)
        out_ref[2 * pair, :, width : width + half] = first.astype(jnp.bfloat16)
        out_ref[2 * pair + 1, :, width : width + half] = second.astype(jnp.bfloat16)
        places = tail_digits[pair * 8 : (pair + 1) * 8, :]
        for odd, tail_part in ((0, places), (1, pltpu.roll(places, 4, 0))):
            partner = 2 * pair + odd
            both = jnp.where(
                left,
                main_digits[partner * 8 : (partner + 1) * 8, :],
                jnp.where(upper_line, 0.0, tail_part),
            )
            out_ref[partner, :, width + half :] = both.astype(jnp.bfloat16)


def score_kernel(got_ref, best_ref, member, digits, earlier_col, row_best, col_best):
    devices, _, total = got_ref.shape
    width = (total - 128) * 2 // 3
    half = width // 2
    main_rows, tail_rows = devices * MAIN, devices * TAIL
    docs = main_rows + tail_rows
    upper_half = lax.broadcasted_iota(jnp.int32, (8, half), 0) >= 4
    upper_line = lax.broadcasted_iota(jnp.int32, (8, 128), 0) >= 4
    lane = lax.broadcasted_iota(jnp.int32, (8, 128), 1)
    left = lane < 4
    for pair in range(devices // 2):
        a = got_ref[2 * pair, :, :].astype(jnp.float32)
        b = got_ref[2 * pair + 1, :, :].astype(jnp.float32)
        at = pair * 16
        member[at : at + 16, :] = jnp.concatenate([a[:, :width], b[:, :width]], axis=0).astype(
            jnp.bfloat16
        )
        a_digits, b_digits = a[:, width + half :], b[:, width + half :]
        digits[at : at + 16, :] = jnp.concatenate(
            [jnp.where(left, a_digits, 0.0), jnp.where(left, b_digits, 0.0)], axis=0
        ).astype(jnp.bfloat16)
    for quad in range(devices // 4):
        folded, places = [], []
        for pair in (2 * quad, 2 * quad + 1):
            a = got_ref[2 * pair, :, width:].astype(jnp.float32)
            b = got_ref[2 * pair + 1, :, width:].astype(jnp.float32)
            a_half, b_half = a[:, :half], b[:, :half]
            low = jnp.where(upper_half, pltpu.roll(b_half, 4, 0), a_half)
            high = jnp.where(upper_half, b_half, pltpu.roll(a_half, 4, 0))
            folded.append(jnp.concatenate([low, high], axis=1))
            both = jnp.where(upper_line, pltpu.roll(b[:, half:], 4, 0), a[:, half:])
            places.append(jnp.where(left, 0.0, both))
        at = main_rows + quad * 16
        member[at : at + 16, :] = jnp.concatenate(folded, axis=0).astype(jnp.bfloat16)
        digits[at : at + 16, :] = jnp.concatenate(places, axis=0).astype(jnp.bfloat16)

    def weights(shape, axis):
        line = lax.broadcasted_iota(jnp.int32, shape, axis)
        digit = line & 3
        weight = jnp.where(
            digit == 0,
            4096.0,
            jnp.where(digit == 1, 64.0, jnp.where(digit == 2, 1.0, -262144.0)),
        )
        return jnp.where(line < 8, weight, 0.0).astype(jnp.bfloat16)

    earlier_col[...] = jnp.dot(
        digits[...], weights((128, 128), 0), preferred_element_type=jnp.float32
    )
    place_row = lax.dot_general(
        weights((8, 128), 1), digits[...], NT, preferred_element_type=jnp.float32
    )
    step = 256
    row_best[...] = jnp.full_like(row_best, -1.0)
    col_best[...] = jnp.full_like(col_best, -1.0)
    for i in range(docs // step):
        mine = slice(i * step, (i + 1) * step)
        column = earlier_col[mine, :]
        for j in range(i + 1):
            theirs = slice(j * step, (j + 1) * step)
            scores = lax.dot_general(
                member[mine, :], member[theirs, :], NT, preferred_element_type=jnp.float32
            )
            best = row_best[mine, :]
            for k in range(step // 128):
                at = j * step + k * 128
                part = scores[:, k * 128 : (k + 1) * 128]
                row = place_row[0:1, at : at + 128]
                earlier = row < column
                best = jnp.maximum(best, jnp.where(earlier, part, -1.0))
                if j != i:
                    other = jnp.where(earlier, -1.0, part)
                    col_best[:, at : at + 128] = jnp.maximum(
                        col_best[:, at : at + 128],
                        jnp.max(other.reshape(step // 8, 8, 128), axis=0),
                    )
            row_best[mine, :] = best

    for block in range(docs // 128):
        at = block * 128
        column = jnp.max(col_best[:, at : at + 128], axis=0, keepdims=True)
        turned = jnp.broadcast_to(column, (128, 128)).T
        best = jnp.max(
            jnp.maximum(row_best[at : at + 128, :], turned), axis=1, keepdims=True
        )
        best = jnp.broadcast_to(best, (128, 128))
        line = lax.broadcasted_iota(jnp.int32, (128, 128), 0)
        lanes = lax.broadcasted_iota(jnp.int32, (128, 128), 1)
        if at < main_rows:
            kept = jnp.where(lanes == (line & 7), best, -2.0).reshape(16, 8, 128)
            best_ref[block * 16 : (block + 1) * 16, :] = jnp.max(kept, axis=1)
        else:
            kept = jnp.where(lanes == (line & 3) + MAIN, best, -2.0).reshape(32, 4, 128)
            first = (at - main_rows) // TAIL
            best_ref[first : first + 32, :] = jnp.maximum(
                best_ref[first : first + 32, :], jnp.max(kept, axis=1)
            )


def pick_kernel(got_ref, label_ref, position_ref, out_ref):
    devices = got_ref.shape[0]
    count = label_ref.shape[1]
    table = got_ref[...].T[:16, :]
    top = table.astype(jnp.bfloat16)
    rest = table - top.astype(jnp.float32)
    middle = rest.astype(jnp.bfloat16)
    low = (rest - middle.astype(jnp.float32)).astype(jnp.bfloat16)
    pick = (
        lax.broadcasted_iota(jnp.int32, (devices, count), 0) == label_ref[...]
    ).astype(jnp.bfloat16)

    def dot(part):
        return jnp.dot(part, pick, preferred_element_type=jnp.float32)

    values = (dot(top) + dot(middle)) + dot(low)
    line = lax.broadcasted_iota(jnp.int32, (16, count), 0)
    out_ref[...] = jnp.sum(
        jnp.where(line == position_ref[...], values, 0.0), axis=0, keepdims=True
    )


def shards(embeddings, labels, order_ids):
    rows, width = embeddings.shape
    devices = lax.axis_size("grp") * lax.axis_size("blk")
    total = width + width // 2 + 128
    docs = devices * (MAIN + TAIL)
    label_row = labels.reshape(1, rows)
    order_row = order_ids.reshape(1, rows)
    partners = 16
    params = pltpu.CompilerParams(vmem_limit_bytes=VMEM_LIMIT)

    def whole(*shape):
        return pl.BlockSpec(shape, lambda *_: (0,) * len(shape))

    outgoing, position = pl.pallas_call(
        place_kernel,
        grid=(devices // partners,),
        in_specs=[whole(rows, width), whole(1, rows), whole(1, rows)],
        out_specs=[
            pl.BlockSpec((partners, 8, total), lambda step: (step, 0, 0)),
            whole(1, rows),
        ],
        out_shape=[
            jax.ShapeDtypeStruct((devices, 8, total), jnp.bfloat16),
            jax.ShapeDtypeStruct((1, rows), jnp.int32),
        ],
        scratch_shapes=[
            pltpu.VMEM((rows, width), jnp.bfloat16),
            pltpu.VMEM((128, rows), jnp.bfloat16),
            pltpu.VMEM((8, rows), jnp.int32),
        ],
        compiler_params=params,
        name="place",
    )(embeddings, label_row, order_row)
    got = lax.all_to_all(outgoing, ("grp", "blk"), split_axis=0, concat_axis=0, tiled=True)
    best = pl.pallas_call(
        score_kernel,
        out_shape=jax.ShapeDtypeStruct((devices, 128), jnp.float32),
        scratch_shapes=[
            pltpu.VMEM((docs, width), jnp.bfloat16),
            pltpu.VMEM((docs, 128), jnp.bfloat16),
            pltpu.VMEM((docs, 128), jnp.float32),
            pltpu.VMEM((docs, 128), jnp.float32),
            pltpu.VMEM((8, docs), jnp.float32),
        ],
        compiler_params=params,
        name="score",
    )(got)
    returned = lax.all_to_all(
        best.reshape(devices, 1, 128), ("grp", "blk"), split_axis=0, concat_axis=0, tiled=True
    ).reshape(devices, 128)
    picked = pl.pallas_call(
        pick_kernel,
        out_shape=jax.ShapeDtypeStruct((1, rows), jnp.float32),
        compiler_params=params,
        name="pick",
    )(returned, label_row, position)
    return picked.reshape(rows)


def solution(mesh):
    placed = (P(("grp", "blk"), None), P(("grp", "blk"), None), P(("grp", "blk")))
    return jax.shard_map(
        shards, mesh=mesh, in_specs=placed, out_specs=P(("grp", "blk")), check_vma=False
    )
```

```python
import jax
import jax.numpy as jnp
from jax import lax
from jax.experimental import pallas as pl
from jax.experimental.pallas import tpu as pltpu
from jax.sharding import PartitionSpec as P

MAIN = 8
TAIL = 4
NT = (((1,), (1,)), ((), ()))
VMEM_LIMIT = 48 * 1024 * 1024


def place_kernel(
    rows_hbm, label_hbm, order_hbm, out_ref, position_ref, label_ref,
    rows, order_ref, unit, digits, slots, pick, sems,
):
    count, width = rows.shape
    devices = out_ref.shape[0]
    half = width // 2
    main_rows = devices * MAIN
    copies = [
        pltpu.make_async_copy(source, target, sems.at[k])
        for k, (source, target) in enumerate(
            ((label_hbm, label_ref), (order_hbm, order_ref), (rows_hbm, rows))
        )
    ]
    for copy in copies:
        copy.start()
    for copy in copies:
        copy.wait()

    labels = label_ref[...]
    carry = jnp.zeros((devices, 128), jnp.float32)
    inner = lax.broadcasted_iota(jnp.int32, (128, 256), 0)
    outer = lax.broadcasted_iota(jnp.int32, (128, 256), 1)
    before = ((inner < outer) | (outer >= 128)).astype(jnp.bfloat16)
    for block in range(count // 128):
        at = slice(block * 128, (block + 1) * 128)
        part = labels[:, at]
        member = lax.broadcasted_iota(jnp.int32, (devices, 128), 0) == part
        sums = jnp.dot(
            member.astype(jnp.bfloat16), before, preferred_element_type=jnp.float32
        )
        rank = jnp.where(member, sums[:, :128] + carry, 0.0)
        carry = carry + sums[:, 128:]
        position = jnp.sum(rank, axis=0, keepdims=True).astype(jnp.int32)
        position_ref[:, at] = position
        slots[0:1, at] = jnp.where(position < MAIN, part * MAIN + position, -1)
        slots[1:2, at] = jnp.where(position < MAIN, -1, part * TAIL + position - MAIN)

    slot = slots[...]
    main_at = lax.broadcasted_iota(jnp.int32, (main_rows, count), 0)
    pick[:main_rows, :] = (main_at == slot[0:1]).astype(jnp.float32).astype(jnp.bfloat16)
    tail_at = lax.broadcasted_iota(jnp.int32, (devices * TAIL, count), 0)
    pick[main_rows:, :] = (tail_at == slot[1:2]).astype(jnp.float32).astype(jnp.bfloat16)

    order = order_ref[...]
    line = lax.broadcasted_iota(jnp.int32, (128, count), 0)
    digit = jnp.where(
        (line == 0) | (line == 4),
        order >> 12,
        jnp.where(
            (line == 1) | (line == 5),
            (order >> 6) & 63,
            jnp.where(
                (line == 2) | (line == 6),
                order & 63,
                jnp.where((line == 3) | (line == 7), 1, 0),
            ),
        ),
    )
    digits[...] = digit.astype(jnp.float32).astype(jnp.bfloat16)
    for block in range(4):
        at = slice(block * count // 4, (block + 1) * count // 4)
        values = rows[at, :].astype(jnp.float32)
        scale = lax.rsqrt(
            jnp.mean(values * values, axis=1, keepdims=True) + 1e-06
        ) * width ** (-0.5)
        unit[at, :] = (values * scale).astype(jnp.bfloat16)

    def upper(n):
        return lax.broadcasted_iota(jnp.int32, (devices // 2, 8, n), 1) >= 4

    main_digits = lax.dot_general(
        pick[:main_rows, :], digits[...], NT, preferred_element_type=jnp.float32
    ).reshape(devices // 2, 2, 8, 128)
    tail_digits = lax.dot_general(
        pick[main_rows:, :], digits[...], NT, preferred_element_type=jnp.float32
    ).reshape(devices // 2, 8, 128)
    left = lax.broadcasted_iota(jnp.int32, (devices // 2, 8, 128), 2) < 4
    places = jnp.stack(
        [
            jnp.where(left, main_digits[:, 0], jnp.where(upper(128), 0.0, tail_digits)),
            jnp.where(
                left,
                main_digits[:, 1],
                jnp.where(upper(128), 0.0, pltpu.roll(tail_digits, 4, 1)),
            ),
        ],
        axis=1,
    )
    out_ref[:, :, width + half :] = places.reshape(devices, 8, 128).astype(jnp.bfloat16)
    step = 256
    for n in range(half // step):
        low_at = slice(n * step, (n + 1) * step)
        high_at = slice(half + n * step, half + (n + 1) * step)
        for at in (low_at, high_at):
            main = jnp.dot(
                pick[:main_rows, :], unit[:, at], preferred_element_type=jnp.float32
            )
            out_ref[:, :, at] = main.reshape(devices, 8, step).astype(jnp.bfloat16)
        low, high = (
            jnp.dot(
                pick[main_rows:, :], unit[:, at], preferred_element_type=jnp.float32
            ).reshape(devices // 2, 8, step)
            for at in (low_at, high_at)
        )
        folded = jnp.stack(
            [
                jnp.where(upper(step), pltpu.roll(high, 4, 1), low),
                jnp.where(upper(step), high, pltpu.roll(low, 4, 1)),
            ],
            axis=1,
        )
        out_ref[:, :, width + n * step : width + (n + 1) * step] = folded.reshape(
            devices, 8, step
        ).astype(jnp.bfloat16)


def score_kernel(got_ref, best_ref, member, digits, earlier_col, row_best, col_best):
    devices, _, total = got_ref.shape
    width = (total - 128) * 2 // 3
    half = width // 2
    main_rows, tail_rows = devices * MAIN, devices * TAIL
    docs = main_rows + tail_rows
    upper_half = lax.broadcasted_iota(jnp.int32, (8, half), 0) >= 4
    upper_line = lax.broadcasted_iota(jnp.int32, (8, 128), 0) >= 4
    lane = lax.broadcasted_iota(jnp.int32, (8, 128), 1)
    left = lane < 4
    for pair in range(devices // 2):
        a = got_ref[2 * pair, :, :].astype(jnp.float32)
        b = got_ref[2 * pair + 1, :, :].astype(jnp.float32)
        at = pair * 16
        member[at : at + 16, :] = jnp.concatenate([a[:, :width], b[:, :width]], axis=0).astype(
            jnp.bfloat16
        )
        a_digits, b_digits = a[:, width + half :], b[:, width + half :]
        digits[at : at + 16, :] = jnp.concatenate(
            [jnp.where(left, a_digits, 0.0), jnp.where(left, b_digits, 0.0)], axis=0
        ).astype(jnp.bfloat16)
    for quad in range(devices // 4):
        folded, places = [], []
        for pair in (2 * quad, 2 * quad + 1):
            a = got_ref[2 * pair, :, width:].astype(jnp.float32)
            b = got_ref[2 * pair + 1, :, width:].astype(jnp.float32)
            a_half, b_half = a[:, :half], b[:, :half]
            low = jnp.where(upper_half, pltpu.roll(b_half, 4, 0), a_half)
            high = jnp.where(upper_half, b_half, pltpu.roll(a_half, 4, 0))
            folded.append(jnp.concatenate([low, high], axis=1))
            both = jnp.where(upper_line, pltpu.roll(b[:, half:], 4, 0), a[:, half:])
            places.append(jnp.where(left, 0.0, both))
        at = main_rows + quad * 16
        member[at : at + 16, :] = jnp.concatenate(folded, axis=0).astype(jnp.bfloat16)
        digits[at : at + 16, :] = jnp.concatenate(places, axis=0).astype(jnp.bfloat16)

    def weights(shape, axis):
        line = lax.broadcasted_iota(jnp.int32, shape, axis)
        digit = line & 3
        weight = jnp.where(
            digit == 0,
            4096.0,
            jnp.where(digit == 1, 64.0, jnp.where(digit == 2, 1.0, -262144.0)),
        )
        return jnp.where(line < 8, weight, 0.0).astype(jnp.bfloat16)

    earlier_col[...] = jnp.dot(
        digits[...], weights((128, 128), 0), preferred_element_type=jnp.float32
    )
    place_row = lax.dot_general(
        weights((8, 128), 1), digits[...], NT, preferred_element_type=jnp.float32
    )
    step = 256
    row_best[...] = jnp.full_like(row_best, -1.0)
    col_best[...] = jnp.full_like(col_best, -1.0)
    for i in range(docs // step):
        mine = slice(i * step, (i + 1) * step)
        column = earlier_col[mine, :]
        for j in range(i + 1):
            theirs = slice(j * step, (j + 1) * step)
            scores = lax.dot_general(
                member[mine, :], member[theirs, :], NT, preferred_element_type=jnp.float32
            )
            best = row_best[mine, :]
            for k in range(step // 128):
                at = j * step + k * 128
                part = scores[:, k * 128 : (k + 1) * 128]
                row = place_row[0:1, at : at + 128]
                earlier = row < column
                best = jnp.maximum(best, jnp.where(earlier, part, -1.0))
                if j != i:
                    other = jnp.where(earlier, -1.0, part)
                    col_best[:, at : at + 128] = jnp.maximum(
                        col_best[:, at : at + 128],
                        jnp.max(other.reshape(step // 8, 8, 128), axis=0),
                    )
            row_best[mine, :] = best

    for block in range(docs // 128):
        at = block * 128
        column = jnp.max(col_best[:, at : at + 128], axis=0, keepdims=True)
        turned = jnp.broadcast_to(column, (128, 128)).T
        best = jnp.max(
            jnp.maximum(row_best[at : at + 128, :], turned), axis=1, keepdims=True
        )
        best = jnp.broadcast_to(best, (128, 128))
        line = lax.broadcasted_iota(jnp.int32, (128, 128), 0)
        lanes = lax.broadcasted_iota(jnp.int32, (128, 128), 1)
        if at < main_rows:
            kept = jnp.where(lanes == (line & 7), best, -2.0).reshape(16, 8, 128)
            best_ref[block * 16 : (block + 1) * 16, :] = jnp.max(kept, axis=1)
        else:
            kept = jnp.where(lanes == (line & 3) + MAIN, best, -2.0).reshape(32, 4, 128)
            first = (at - main_rows) // TAIL
            best_ref[first : first + 32, :] = jnp.maximum(
                best_ref[first : first + 32, :], jnp.max(kept, axis=1)
            )


def pick_kernel(got_ref, label_ref, position_ref, out_ref):
    devices = got_ref.shape[0]
    count = label_ref.shape[1]
    table = got_ref[...].T[:16, :]
    top = table.astype(jnp.bfloat16)
    rest = table - top.astype(jnp.float32)
    middle = rest.astype(jnp.bfloat16)
    low = (rest - middle.astype(jnp.float32)).astype(jnp.bfloat16)
    pick = (
        lax.broadcasted_iota(jnp.int32, (devices, count), 0) == label_ref[...]
    ).astype(jnp.bfloat16)

    def dot(part):
        return jnp.dot(part, pick, preferred_element_type=jnp.float32)

    values = (dot(top) + dot(middle)) + dot(low)
    line = lax.broadcasted_iota(jnp.int32, (16, count), 0)
    out_ref[...] = jnp.sum(
        jnp.where(line == position_ref[...], values, 0.0), axis=0, keepdims=True
    )


def shards(embeddings, labels, order_ids):
    rows, width = embeddings.shape
    devices = lax.axis_size("grp") * lax.axis_size("blk")
    total = width + width // 2 + 128
    docs = devices * (MAIN + TAIL)
    params = pltpu.CompilerParams(vmem_limit_bytes=VMEM_LIMIT)
    in_hbm = pl.BlockSpec(memory_space=pltpu.HBM)
    outgoing, position, label_row = pl.pallas_call(
        place_kernel,
        in_specs=[in_hbm] * 3,
        out_shape=[
            jax.ShapeDtypeStruct((devices, 8, total), jnp.bfloat16),
            jax.ShapeDtypeStruct((1, rows), jnp.int32),
            jax.ShapeDtypeStruct((1, rows), jnp.int32),
        ],
        scratch_shapes=[
            pltpu.VMEM((rows, width), jnp.bfloat16),
            pltpu.VMEM((1, rows), jnp.int32),
            pltpu.VMEM((rows, width), jnp.bfloat16),
            pltpu.VMEM((128, rows), jnp.bfloat16),
            pltpu.VMEM((8, rows), jnp.int32),
            pltpu.VMEM((docs, rows), jnp.bfloat16),
            pltpu.SemaphoreType.DMA((3,)),
        ],
        compiler_params=params,
        name="place",
    )(
        *(
            pltpu.with_memory_space_constraint(x, pltpu.HBM)
            for x in (embeddings, labels.reshape(1, rows), order_ids.reshape(1, rows))
        )
    )
    got = lax.all_to_all(outgoing, ("grp", "blk"), split_axis=0, concat_axis=0, tiled=True)
    best = pl.pallas_call(
        score_kernel,
        out_shape=jax.ShapeDtypeStruct((devices, 128), jnp.float32),
        scratch_shapes=[
            pltpu.VMEM((docs, width), jnp.bfloat16),
            pltpu.VMEM((docs, 128), jnp.bfloat16),
            pltpu.VMEM((docs, 128), jnp.float32),
            pltpu.VMEM((docs, 128), jnp.float32),
            pltpu.VMEM((8, docs), jnp.float32),
        ],
        compiler_params=params,
        name="score",
    )(got)
    returned = lax.all_to_all(
        best.reshape(devices, 1, 128), ("grp", "blk"), split_axis=0, concat_axis=0, tiled=True
    ).reshape(devices, 128)
    picked = pl.pallas_call(
        pick_kernel,
        out_shape=jax.ShapeDtypeStruct((1, rows), jnp.float32),
        compiler_params=params,
        name="pick",
    )(returned, label_row, position)
    return picked.reshape(rows)


def solution(mesh):
    placed = (P(("grp", "blk"), None), P(("grp", "blk"), None), P(("grp", "blk")))
    return jax.shard_map(
        shards, mesh=mesh, in_specs=placed, out_specs=P(("grp", "blk")), check_vma=False
    )
```

```python
import jax
import jax.numpy as jnp
from jax import lax
from jax.experimental import pallas as pl
from jax.experimental.pallas import tpu as pltpu
from jax.sharding import PartitionSpec as P

MAIN = 8
TAIL = 4
CAP = MAIN + TAIL
GROUP = 4
TURNS = (0, 2, 1, 3)
NT = (((1,), (1,)), ((), ()))
VMEM_LIMIT = 48 * 1024 * 1024


def place_kernel(
    rows_hbm, label_hbm, order_hbm, out_ref, position_ref, label_ref,
    rows, order_ref, unit, slots, pick, sems,
):
    count, width = rows.shape
    groups = out_ref.shape[0]
    devices = groups * GROUP
    half = width // 2
    main_rows, tail_rows = devices * MAIN, devices * TAIL
    parts = 4
    part_rows = count // parts
    small = [
        pltpu.make_async_copy(source, target, sems.at[parts + k])
        for k, (source, target) in enumerate(((label_hbm, label_ref), (order_hbm, order_ref)))
    ]
    large = []
    for k in range(parts):
        at = pl.ds(k * part_rows, part_rows)
        large.append(pltpu.make_async_copy(rows_hbm.at[at, :], rows.at[at, :], sems.at[k]))
    for copy in small + large:
        copy.start()
    for copy in small:
        copy.wait()

    labels = label_ref[...]
    carry = jnp.zeros((devices, 128), jnp.float32)
    inner = lax.broadcasted_iota(jnp.int32, (128, 256), 0)
    outer = lax.broadcasted_iota(jnp.int32, (128, 256), 1)
    before = ((inner < outer) | (outer >= 128)).astype(jnp.bfloat16)
    for block in range(count // 128):
        at = slice(block * 128, (block + 1) * 128)
        part = labels[:, at]
        member = lax.broadcasted_iota(jnp.int32, (devices, 128), 0) == part
        sums = jnp.dot(
            member.astype(jnp.bfloat16), before, preferred_element_type=jnp.float32
        )
        rank = jnp.where(member, sums[:, :128] + carry, 0.0)
        carry = carry + sums[:, 128:]
        position = jnp.sum(rank, axis=0, keepdims=True).astype(jnp.int32)
        position_ref[:, at] = position
        slots[0:1, at] = jnp.where(position < MAIN, part * MAIN + position, -1)
        slots[1:2, at] = jnp.where(position < MAIN, -1, part * TAIL + position - MAIN)
    for copy in large:
        copy.wait()

    slot = slots[...]
    main_pick = lax.broadcasted_iota(jnp.int32, (main_rows, count), 0) == slot[0:1]
    pick[:main_rows, :] = main_pick.astype(jnp.float32).astype(jnp.bfloat16)
    tail_pick = lax.broadcasted_iota(jnp.int32, (tail_rows, count), 0) == slot[1:2]
    pick[main_rows:, :] = tail_pick.astype(jnp.float32).astype(jnp.bfloat16)

    for k in range(parts):
        at = slice(k * part_rows, (k + 1) * part_rows)
        values = rows[at, :].astype(jnp.float32)
        scale = lax.rsqrt(
            jnp.mean(values * values, axis=1, keepdims=True) + 1e-06
        ) * width ** (-0.5)
        unit[at, :] = (values * scale).astype(jnp.bfloat16)

    key = (order_ref[...] + 262144).astype(jnp.float32)

    def digits(chosen, row):
        found = jnp.where(
            lax.broadcasted_iota(jnp.int32, (chosen, count), 0) == row,
            jnp.broadcast_to(key, (chosen, count)),
            0.0,
        )
        total = found[:, :128]
        for block in range(1, count // 128):
            total = total + found[:, block * 128 : (block + 1) * 128]
        total = jnp.sum(total, axis=1, keepdims=True).astype(jnp.int32)
        total = jnp.broadcast_to(total, (chosen, 128))
        digit = lax.broadcasted_iota(jnp.int32, (chosen, 128), 1) & 3
        shift = jnp.where(
            digit == 0, 12, jnp.where(digit == 1, 6, jnp.where(digit == 2, 0, 18))
        )
        return ((total >> shift) & 63).astype(jnp.float32)

    line = lax.broadcasted_iota(jnp.int32, (1, 8, 128), 1)
    owner = lax.broadcasted_iota(jnp.int32, (1, 8, 128), 2) >> 2
    main_digits = digits(main_rows, slot[0:1]).reshape(devices, 8, 128)
    places = jnp.sum(jnp.where(owner == line, main_digits, 0.0), axis=1, keepdims=True)
    tail_digits = digits(tail_rows, slot[1:2]).reshape(devices // 2, 8, 128)
    mine = owner == (line & 3) + MAIN
    tail_places = jnp.stack(
        [
            jnp.sum(jnp.where(mine & (line < 4), tail_digits, 0.0), axis=1, keepdims=True),
            jnp.sum(jnp.where(mine & (line >= 4), tail_digits, 0.0), axis=1, keepdims=True),
        ],
        axis=1,
    ).reshape(devices, 1, 128)
    places = jnp.broadcast_to(places + tail_places, (devices, 8, 128))
    places = places.reshape(groups, GROUP, 8, 128)

    def put(tile, values):
        values = values.reshape(groups, GROUP, 8, 128)
        if tile:
            for e in range(GROUP):
                out_ref[:, CAP * e + tile] = values[:, e].astype(jnp.bfloat16)
            return
        out_ref[:, 0] = values[:, 0].astype(jnp.bfloat16)
        turn = line >> 1
        for e in range(1, GROUP + 1):
            mixed = jnp.where(turn == e - 1, places[:, e - 1], values[:, e - 1])
            if e < GROUP:
                mixed = jnp.where(turn >= e, values[:, e], mixed)
            out_ref[:, CAP * e] = mixed.astype(jnp.bfloat16)

    step = 256
    upper = lax.broadcasted_iota(jnp.int32, (devices // 2, 8, step), 1) >= 4
    for n in range(half // step):
        ends = (n * step, half + n * step)
        for first in ends:
            main = jnp.dot(
                pick[:main_rows, :],
                unit[:, first : first + step],
                preferred_element_type=jnp.float32,
            )
            for k in range(step // 128):
                put(first // 128 + k, main[:, k * 128 : (k + 1) * 128])
        low, high = (
            jnp.dot(
                pick[main_rows:, :],
                unit[:, first : first + step],
                preferred_element_type=jnp.float32,
            ).reshape(devices // 2, 8, step)
            for first in ends
        )
        folded = jnp.stack(
            [
                jnp.where(upper, pltpu.roll(high, 4, 1), low),
                jnp.where(upper, high, pltpu.roll(low, 4, 1)),
            ],
            axis=1,
        ).reshape(devices, 8, step)
        for k in range(step // 128):
            put(MAIN + n * step // 128 + k, folded[:, :, k * 128 : (k + 1) * 128])


def score_kernel(got_ref, best_ref, member, digits, column, row_best, col_best, results):
    groups = got_ref.shape[0]
    devices = groups * GROUP
    docs, width = member.shape
    pieces = width // 128
    main_rows = devices * MAIN
    last = GROUP * CAP
    me = lax.axis_index("blk")
    line = lax.broadcasted_iota(jnp.int32, (8, 128), 0)
    lane = lax.broadcasted_iota(jnp.int32, (8, 128), 1)
    turn, owner = line >> 1, lane >> 2
    inner = (turn == 1) | (turn == 2)
    first_half = turn < 2

    def both(a, b):
        return jnp.concatenate([a, b], axis=0).astype(jnp.bfloat16)

    for group in range(groups):
        chunks = []
        for turns in range(GROUP):
            source = (me + turns) & 3
            base = CAP * source - jnp.where(source < me, 1, 0)
            tiles = [
                got_ref[group, jnp.clip(base + t, 0, last)].astype(jnp.float32)
                for t in range(CAP + 2)
            ]
            if turns:
                tiles = [
                    jnp.where(turn >= turns, tiles[t], tiles[t + 1]) for t in range(CAP + 1)
                ]
            tiles[0] = jnp.where(((turn - turns) & 3) >= me, tiles[0], tiles[CAP])
            chunks.append(tiles)
        places = got_ref[group, last].astype(jnp.float32)
        for e in range(GROUP - 1):
            places = jnp.where(
                turn == e, got_ref[group, CAP * (e + 1)].astype(jnp.float32), places
            )
        places = pltpu.roll(places, (8 - 2 * me) & 7, 0)
        places = [
            jnp.broadcast_to(places[2 * turns : 2 * turns + 1, :], (8, 128))
            for turns in range(GROUP)
        ]
        for k in range(2):
            a, b = TURNS[2 * k], TURNS[2 * k + 1]
            at = slice(group * 32 + k * 16, group * 32 + k * 16 + 16)
            for t in range(pieces):
                member[at, t * 128 : (t + 1) * 128] = both(chunks[a][t], chunks[b][t])
            digits[at, :] = both(
                *(
                    jnp.where(owner == ((line - 2 * turns) & 7), places[turns], 0.0)
                    for turns in (a, b)
                )
            )
        at = slice(main_rows + group * 16, main_rows + group * 16 + 16)
        for t in range(pieces // 2):
            a, b, c, d = (chunks[turns][MAIN + t] for turns in range(GROUP))
            member[at, t * 128 : (t + 1) * 128] = both(
                jnp.where(first_half, a, c), jnp.where(inner, b, d)
            )
            t = t + pieces // 2
            member[at, t * 128 : (t + 1) * 128] = both(
                pltpu.roll(jnp.where(first_half, c, a), 4, 0),
                pltpu.roll(jnp.where(inner, d, b), 4, 0),
            )
        digits[at, :] = both(
            jnp.where(
                owner == MAIN + (line & 3), jnp.where(first_half, places[0], places[2]), 0.0
            ),
            jnp.where(
                owner == MAIN + ((line - 2) & 3), jnp.where(inner, places[1], places[3]), 0.0
            ),
        )

    def weights(shape, axis):
        at = lax.broadcasted_iota(jnp.int32, shape, axis)
        digit = at & 3
        weight = jnp.where(
            digit == 0,
            4096.0,
            jnp.where(digit == 1, 64.0, jnp.where(digit == 2, 1.0, -262144.0)),
        )
        return jnp.where(at < 4 * CAP, weight, 0.0).astype(jnp.bfloat16)

    column[...] = jnp.dot(
        digits[...], weights((128, 128), 0), preferred_element_type=jnp.float32
    )
    place_row = lax.dot_general(
        weights((8, 128), 1), digits[...], NT, preferred_element_type=jnp.float32
    )
    step = 256
    col_best[...] = jnp.full_like(col_best, -1.0)
    for i in range(docs // step):
        mine = slice(i * step, (i + 1) * step)
        best = jnp.full((step, 128), -1.0, jnp.float32)
        for j in range(i + 1):
            theirs = slice(j * step, (j + 1) * step)
            scores = lax.dot_general(
                member[mine, :], member[theirs, :], NT, preferred_element_type=jnp.float32
            )
            for k in range(step // 128):
                at = j * step + k * 128
                part = scores[:, k * 128 : (k + 1) * 128]
                earlier = place_row[0:1, at : at + 128] < column[mine, :]
                best = jnp.maximum(best, jnp.where(earlier, part, -1.0))
                if j != i:
                    other = jnp.where(earlier, -1.0, part)
                    col_best[:, at : at + 128] = jnp.maximum(
                        col_best[:, at : at + 128],
                        jnp.max(other.reshape(step // 8, 8, 128), axis=0),
                    )
        row_best[mine, :] = jnp.broadcast_to(
            jnp.max(best, axis=1, keepdims=True), (step, 128)
        )

    line = lax.broadcasted_iota(jnp.int32, (128, 128), 0)
    lane = lax.broadcasted_iota(jnp.int32, (128, 128), 1)
    for block in range(docs // 128):
        at = block * 128
        best = jnp.maximum(
            row_best[at : at + 128, :],
            jnp.broadcast_to(
                jnp.max(col_best[:, at : at + 128].T, axis=1, keepdims=True), (128, 128)
            ),
        )
        if at < main_rows:
            index = (line >> 3) & 3
            turns = jnp.where(index == 1, 2, jnp.where(index == 2, 1, index))
            kept = jnp.where(lane == ((line - 2 * turns) & 7), best, -2.0)
            results[block * 16 : (block + 1) * 16, :] = jnp.max(
                kept.reshape(16, 8, 128), axis=1
            )
        else:
            odd = ((line >> 3) & 1) * 2
            kept = jnp.where(lane == MAIN + ((line - odd) & 3), best, -2.0)
            kept = kept.reshape(8, 2, 8, 128)
            row = lax.broadcasted_iota(jnp.int32, (8, 8, 128), 1)
            first = (at - main_rows) // TAIL
            for index in range(GROUP):
                start = (0, 4, 2, 6)[index]
                mine = ((row - start) & 7) < 4
                found = jnp.max(jnp.where(mine, kept[:, index // 2], -2.0), axis=1)
                where = pl.ds(first + index, 8, stride=GROUP)
                results[where, :] = jnp.maximum(results[where, :], found)
    for index, turns in enumerate(TURNS):
        best_ref[pl.ds((me + turns) & 3, groups, stride=GROUP), :] = results[
            pl.ds(index, groups, stride=GROUP), :
        ]


def pick_kernel(got_ref, label_ref, position_ref, out_ref):
    devices = got_ref.shape[0]
    count = label_ref.shape[1]
    table = got_ref[...].T[:16, :]
    top = table.astype(jnp.bfloat16)
    rest = table - top.astype(jnp.float32)
    middle = rest.astype(jnp.bfloat16)
    low = (rest - middle.astype(jnp.float32)).astype(jnp.bfloat16)
    pick = (
        lax.broadcasted_iota(jnp.int32, (devices, count), 0) == label_ref[...]
    ).astype(jnp.bfloat16)

    def dot(part):
        return jnp.dot(part, pick, preferred_element_type=jnp.float32)

    values = (dot(top) + dot(middle)) + dot(low)
    line = lax.broadcasted_iota(jnp.int32, (16, count), 0)
    out_ref[...] = jnp.sum(
        jnp.where(line == position_ref[...], values, 0.0), axis=0, keepdims=True
    )


def shards(embeddings, labels, order_ids):
    rows, width = embeddings.shape
    devices = lax.axis_size("grp") * lax.axis_size("blk")
    groups, units = devices // GROUP, GROUP * CAP + 1
    docs = devices * CAP
    params = pltpu.CompilerParams(vmem_limit_bytes=VMEM_LIMIT)
    in_hbm = pl.BlockSpec(memory_space=pltpu.HBM)
    outgoing, position, label_row = pl.pallas_call(
        place_kernel,
        in_specs=[in_hbm] * 3,
        out_shape=[
            jax.ShapeDtypeStruct((groups, units, 8, 128), jnp.bfloat16),
            jax.ShapeDtypeStruct((1, rows), jnp.int32),
            jax.ShapeDtypeStruct((1, rows), jnp.int32),
        ],
        scratch_shapes=[
            pltpu.VMEM((rows, width), jnp.bfloat16),
            pltpu.VMEM((1, rows), jnp.int32),
            pltpu.VMEM((rows, width), jnp.bfloat16),
            pltpu.VMEM((8, rows), jnp.int32),
            pltpu.VMEM((docs, rows), jnp.bfloat16),
            pltpu.SemaphoreType.DMA((6,)),
        ],
        compiler_params=params,
        name="place",
    )(
        *(
            pltpu.with_memory_space_constraint(x, pltpu.HBM)
            for x in (embeddings, labels.reshape(1, rows), order_ids.reshape(1, rows))
        )
    )
    got = lax.all_to_all(
        outgoing.reshape(devices, units, 2, 128),
        ("grp", "blk"),
        split_axis=0,
        concat_axis=0,
        tiled=True,
    )
    best = pl.pallas_call(
        score_kernel,
        out_shape=jax.ShapeDtypeStruct((devices, 128), jnp.float32),
        scratch_shapes=[
            pltpu.VMEM((docs, width), jnp.bfloat16),
            pltpu.VMEM((docs, 128), jnp.bfloat16),
            pltpu.VMEM((docs, 128), jnp.float32),
            pltpu.VMEM((docs, 128), jnp.float32),
            pltpu.VMEM((8, docs), jnp.float32),
            pltpu.VMEM((devices, 128), jnp.float32),
        ],
        compiler_params=params,
        name="score",
    )(got.reshape(groups, units, 8, 128))
    returned = lax.all_to_all(
        best.reshape(devices, 1, 128), ("grp", "blk"), split_axis=0, concat_axis=0, tiled=True
    ).reshape(devices, 128)
    picked = pl.pallas_call(
        pick_kernel,
        out_shape=jax.ShapeDtypeStruct((1, rows), jnp.float32),
        compiler_params=params,
        name="pick",
    )(returned, label_row, position)
    return picked.reshape(rows)


def solution(mesh):
    placed = (P(("grp", "blk"), None), P(("grp", "blk"), None), P(("grp", "blk")))
    return jax.shard_map(
        shards, mesh=mesh, in_specs=placed, out_specs=P(("grp", "blk")), check_vma=False
    )
```

```python
import jax
import jax.numpy as jnp
from jax import lax
from jax.experimental import pallas as pl
from jax.experimental.pallas import tpu as pltpu
from jax.sharding import PartitionSpec as P

MAIN = 8
TAIL = 4
CAP = MAIN + TAIL
GROUP = 4
TURNS = (0, 2, 1, 3)
NT = (((1,), (1,)), ((), ()))
VMEM_LIMIT = 48 * 1024 * 1024


def place_kernel(
    rows_hbm, label_hbm, order_hbm, out_ref, lane_ref, label_ref,
    rows, order_ref, unit, pick, members, marks, places, sems,
):
    count, width = rows.shape
    groups = out_ref.shape[0]
    devices = groups * GROUP
    half = width // 2
    main_rows, tail_rows = devices * MAIN, devices * TAIL
    parts = 4
    part_rows = count // parts
    copies = [
        pltpu.make_async_copy(source, target, sems.at[parts + k])
        for k, (source, target) in enumerate(((label_hbm, label_ref), (order_hbm, order_ref)))
    ]
    large = []
    for k in range(parts):
        at = pl.ds(k * part_rows, part_rows)
        large.append(pltpu.make_async_copy(rows_hbm.at[at, :], rows.at[at, :], sems.at[k]))
    for copy in copies + large:
        copy.start()
    for copy in copies:
        copy.wait()

    me = lax.axis_index("blk")
    labels = label_ref[...]
    carry = jnp.zeros((devices, 128), jnp.float32)
    inner = lax.broadcasted_iota(jnp.int32, (128, 256), 0)
    outer = lax.broadcasted_iota(jnp.int32, (128, 256), 1)
    before = ((inner < outer) | (outer >= 128)).astype(jnp.bfloat16)
    slot_of = lax.broadcasted_iota(jnp.int32, (128, 128), 0) >> 2
    digit_of = lax.broadcasted_iota(jnp.int32, (128, 128), 0) & 3
    shift = jnp.where(
        digit_of == 0, 12, jnp.where(digit_of == 1, 6, jnp.where(digit_of == 2, 0, 18))
    )
    positions = []
    for block in range(count // 128):
        at = slice(block * 128, (block + 1) * 128)
        part = labels[:, at]
        member = lax.broadcasted_iota(jnp.int32, (devices, 128), 0) == part
        ones = member.astype(jnp.float32).astype(jnp.bfloat16)
        members[:, at] = ones
        sums = jnp.dot(ones, before, preferred_element_type=jnp.float32)
        rank = jnp.where(member, sums[:, :128] + carry, 0.0)
        carry = carry + sums[:, 128:]
        position = jnp.sum(rank, axis=0, keepdims=True).astype(jnp.int32)
        positions.append(position)
        turned = (position + 2 * ((me - part) & 3)) & 7
        lane_ref[:, at] = jnp.where(position < MAIN, turned, MAIN + turned)
        digit = ((order_ref[:, at] + 262144) >> shift) & 63
        marks[:, at] = (
            jnp.where(slot_of == position, digit, 0).astype(jnp.float32).astype(jnp.bfloat16)
        )
    for copy in large:
        copy.wait()

    position = jnp.concatenate(positions, axis=1)
    index = lax.broadcasted_iota(jnp.int32, (128, 128), 0).astype(jnp.float32)
    index = jnp.concatenate([index.astype(jnp.bfloat16)] * (count // 128), axis=1)
    index = index.reshape(8, 16, count)
    one, zero = jnp.ones((), jnp.bfloat16), jnp.zeros((), jnp.bfloat16)

    def choose(first, chosen, code):
        code = jnp.where(chosen, code, -1).astype(jnp.float32)
        code = jnp.broadcast_to(code, (16, count)).astype(jnp.bfloat16)
        pick[first : first + 128, :] = jnp.where(index == code[None], one, zero).reshape(
            128, count
        )

    for block in range(main_rows // 128):
        choose(
            block * 128,
            ((labels >> 4) == block) & (position < MAIN),
            (labels & 15) * MAIN + position,
        )
    for block in range(tail_rows // 128):
        choose(
            main_rows + block * 128,
            ((labels >> 5) == block) & (position >= MAIN),
            (labels & 31) * TAIL + position - MAIN,
        )
    places[...] = lax.dot_general(
        members[...], marks[...], NT, preferred_element_type=jnp.float32
    )

    for k in range(parts):
        at = slice(k * part_rows, (k + 1) * part_rows)
        values = rows[at, :].astype(jnp.float32)
        scale = lax.rsqrt(
            jnp.mean(values * values, axis=1, keepdims=True) + 1e-06
        ) * width ** (-0.5)
        unit[at, :] = (values * scale).astype(jnp.bfloat16)

    turn = lax.broadcasted_iota(jnp.int32, (8, 128), 0) >> 1

    def put(tile, values):
        values = values.reshape(groups, GROUP, 8, 128)
        if tile:
            for e in range(GROUP):
                out_ref[:, CAP * e + tile] = values[:, e].astype(jnp.bfloat16)
            return
        for group in range(groups):
            out_ref[group, 0] = values[group, 0].astype(jnp.bfloat16)
            for e in range(1, GROUP + 1):
                at = group * GROUP + e - 1
                mixed = jnp.where(
                    turn == e - 1,
                    jnp.broadcast_to(places[at : at + 1, :], (8, 128)),
                    values[group, e - 1],
                )
                if e < GROUP:
                    mixed = jnp.where(turn >= e, values[group, e], mixed)
                out_ref[group, CAP * e] = mixed.astype(jnp.bfloat16)

    step = 256
    upper = lax.broadcasted_iota(jnp.int32, (devices // 2, 8, step), 1) >= 4
    for n in range(half // step):
        ends = (n * step, half + n * step)
        for first in ends:
            main = jnp.dot(
                pick[:main_rows, :],
                unit[:, first : first + step],
                preferred_element_type=jnp.float32,
            )
            for k in range(step // 128):
                put(first // 128 + k, main[:, k * 128 : (k + 1) * 128])
        low, high = (
            jnp.dot(
                pick[main_rows:, :],
                unit[:, first : first + step],
                preferred_element_type=jnp.float32,
            ).reshape(devices // 2, 8, step)
            for first in ends
        )
        folded = jnp.stack(
            [
                jnp.where(upper, pltpu.roll(high, 4, 1), low),
                jnp.where(upper, high, pltpu.roll(low, 4, 1)),
            ],
            axis=1,
        ).reshape(devices, 8, step)
        for k in range(step // 128):
            put(MAIN + n * step // 128 + k, folded[:, :, k * 128 : (k + 1) * 128])


def score_kernel(got_ref, best_ref, member, digits, column, row_best, col_best, results):
    groups = got_ref.shape[0]
    devices = groups * GROUP
    docs, width = member.shape
    pieces = width // 128
    main_rows = devices * MAIN
    last = GROUP * CAP
    me = lax.axis_index("blk")
    line = lax.broadcasted_iota(jnp.int32, (8, 128), 0)
    lane = lax.broadcasted_iota(jnp.int32, (8, 128), 1)
    turn, owner = line >> 1, lane >> 2
    inner = (turn == 1) | (turn == 2)
    first_half = turn < 2

    def both(a, b):
        return jnp.concatenate([a, b], axis=0).astype(jnp.bfloat16)

    for group in range(groups):
        chunks = []
        for turns in range(GROUP):
            source = (me + turns) & 3
            base = CAP * source - jnp.where(source < me, 1, 0)
            tiles = [
                got_ref[group, jnp.clip(base + t, 0, last)].astype(jnp.float32)
                for t in range(CAP + 2)
            ]
            if turns:
                tiles = [
                    jnp.where(turn >= turns, tiles[t], tiles[t + 1]) for t in range(CAP + 1)
                ]
            tiles[0] = jnp.where(((turn - turns) & 3) >= me, tiles[0], tiles[CAP])
            chunks.append(tiles)
        places = got_ref[group, last].astype(jnp.float32)
        for e in range(GROUP - 1):
            places = jnp.where(
                turn == e, got_ref[group, CAP * (e + 1)].astype(jnp.float32), places
            )
        places = pltpu.roll(places, (8 - 2 * me) & 7, 0)
        places = [
            jnp.broadcast_to(places[2 * turns : 2 * turns + 1, :], (8, 128))
            for turns in range(GROUP)
        ]
        for k in range(2):
            a, b = TURNS[2 * k], TURNS[2 * k + 1]
            at = slice(group * 32 + k * 16, group * 32 + k * 16 + 16)
            for t in range(pieces):
                member[at, t * 128 : (t + 1) * 128] = both(chunks[a][t], chunks[b][t])
            digits[at, :] = both(
                *(
                    jnp.where(owner == ((line - 2 * turns) & 7), places[turns], 0.0)
                    for turns in (a, b)
                )
            )
        at = slice(main_rows + group * 16, main_rows + group * 16 + 16)
        for t in range(pieces // 2):
            a, b, c, d = (chunks[turns][MAIN + t] for turns in range(GROUP))
            member[at, t * 128 : (t + 1) * 128] = both(
                jnp.where(first_half, a, c), jnp.where(inner, b, d)
            )
            t = t + pieces // 2
            member[at, t * 128 : (t + 1) * 128] = both(
                pltpu.roll(jnp.where(first_half, c, a), 4, 0),
                pltpu.roll(jnp.where(inner, d, b), 4, 0),
            )
        digits[at, :] = both(
            jnp.where(
                owner == MAIN + (line & 3), jnp.where(first_half, places[0], places[2]), 0.0
            ),
            jnp.where(
                owner == MAIN + ((line - 2) & 3), jnp.where(inner, places[1], places[3]), 0.0
            ),
        )

    def weights(shape, axis):
        at = lax.broadcasted_iota(jnp.int32, shape, axis)
        digit = at & 3
        weight = jnp.where(
            digit == 0,
            4096.0,
            jnp.where(digit == 1, 64.0, jnp.where(digit == 2, 1.0, -262144.0)),
        )
        return jnp.where(at < 4 * CAP, weight, 0.0).astype(jnp.bfloat16)

    column[...] = jnp.dot(
        digits[...], weights((128, 128), 0), preferred_element_type=jnp.float32
    )
    place_row = lax.dot_general(
        weights((8, 128), 1), digits[...], NT, preferred_element_type=jnp.float32
    )
    step = 256
    col_best[...] = jnp.full_like(col_best, -1.0)
    for i in range(docs // step):
        mine = slice(i * step, (i + 1) * step)
        best = jnp.full((step, 128), -1.0, jnp.float32)
        for j in range(i + 1):
            theirs = slice(j * step, (j + 1) * step)
            scores = lax.dot_general(
                member[mine, :], member[theirs, :], NT, preferred_element_type=jnp.float32
            )
            for k in range(step // 128):
                at = j * step + k * 128
                part = scores[:, k * 128 : (k + 1) * 128]
                earlier = place_row[0:1, at : at + 128] < column[mine, :]
                best = jnp.maximum(best, jnp.where(earlier, part, -1.0))
                if j != i:
                    other = jnp.where(earlier, -1.0, part)
                    col_best[:, at : at + 128] = jnp.maximum(
                        col_best[:, at : at + 128],
                        jnp.max(other.reshape(step // 8, 8, 128), axis=0),
                    )
        best = jnp.broadcast_to(jnp.max(best, axis=1, keepdims=True), (step, 128))
        place = lax.broadcasted_iota(jnp.int32, (step, 128), 0) & 7
        if i * step >= main_rows:
            place = place + MAIN
        best = jnp.where(lax.broadcasted_iota(jnp.int32, (step, 128), 1) == place, best, -2.0)
        row_best[i * step // 8 : (i + 1) * step // 8, :] = jnp.max(
            best.reshape(step // 8, 8, 128), axis=1
        )

    own = (
        lax.broadcasted_iota(jnp.int32, (16, 128), 1) >> 3
        == lax.broadcasted_iota(jnp.int32, (16, 128), 0)
    )
    for block in range(docs // 128):
        best = jnp.max(col_best[:, block * 128 : (block + 1) * 128], axis=0, keepdims=True)
        best = jnp.where(own, jnp.broadcast_to(best, (16, 128)), -2.0)
        for shift in (64, 32, 16, 8):
            best = jnp.maximum(best, pltpu.roll(best, shift, 1))
        at = slice(block * 16, (block + 1) * 16)
        results[at, :] = jnp.maximum(best, row_best[at, :])
    lane = lax.broadcasted_iota(jnp.int32, (groups, 128), 1)
    for index, turns in enumerate(TURNS):
        best_ref[pl.ds((me + turns) & 3, groups, stride=GROUP), :] = jnp.where(
            lane < MAIN,
            results[pl.ds(index, groups, stride=GROUP), :],
            results[pl.ds(devices + index // 2, groups, stride=2), :],
        )


def pick_kernel(got_ref, label_ref, lane_ref, out_ref):
    devices = got_ref.shape[0]
    count = label_ref.shape[1]
    table = got_ref[...].T[: 2 * MAIN, :]
    top = table.astype(jnp.bfloat16).astype(jnp.float32)
    rest = table - top
    middle = rest.astype(jnp.bfloat16).astype(jnp.float32)
    parts = jnp.concatenate([top, middle, rest - middle], axis=0).astype(jnp.bfloat16)
    chosen = lax.broadcasted_iota(jnp.int32, (devices, count), 0) == label_ref[...]
    values = jnp.dot(
        parts,
        chosen.astype(jnp.float32).astype(jnp.bfloat16),
        preferred_element_type=jnp.float32,
    )
    values = (values[: 2 * MAIN] + values[2 * MAIN : 4 * MAIN]) + values[4 * MAIN :]
    line = lax.broadcasted_iota(jnp.int32, (2 * MAIN, count), 0)
    out_ref[...] = jnp.sum(
        jnp.where(line == lane_ref[...], values, 0.0), axis=0, keepdims=True
    )


def shards(embeddings, labels, order_ids):
    rows, width = embeddings.shape
    devices = lax.axis_size("grp") * lax.axis_size("blk")
    groups, units = devices // GROUP, GROUP * CAP + 1
    docs = devices * CAP
    params = pltpu.CompilerParams(vmem_limit_bytes=VMEM_LIMIT)
    in_hbm = pl.BlockSpec(memory_space=pltpu.HBM)
    outgoing, lane_row, label_row = pl.pallas_call(
        place_kernel,
        in_specs=[in_hbm] * 3,
        out_shape=[
            jax.ShapeDtypeStruct((groups, units, 8, 128), jnp.bfloat16),
            jax.ShapeDtypeStruct((1, rows), jnp.int32),
            jax.ShapeDtypeStruct((1, rows), jnp.int32),
        ],
        scratch_shapes=[
            pltpu.VMEM((rows, width), jnp.bfloat16),
            pltpu.VMEM((1, rows), jnp.int32),
            pltpu.VMEM((rows, width), jnp.bfloat16),
            pltpu.VMEM((docs, rows), jnp.bfloat16),
            pltpu.VMEM((devices, rows), jnp.bfloat16),
            pltpu.VMEM((128, rows), jnp.bfloat16),
            pltpu.VMEM((devices, 128), jnp.float32),
            pltpu.SemaphoreType.DMA((6,)),
        ],
        compiler_params=params,
        name="place",
    )(
        *(
            pltpu.with_memory_space_constraint(x, pltpu.HBM)
            for x in (embeddings, labels.reshape(1, rows), order_ids.reshape(1, rows))
        )
    )
    got = lax.all_to_all(
        outgoing.reshape(devices, units, 2, 128),
        ("grp", "blk"),
        split_axis=0,
        concat_axis=0,
        tiled=True,
    )
    best = pl.pallas_call(
        score_kernel,
        out_shape=jax.ShapeDtypeStruct((devices, 128), jnp.float32),
        scratch_shapes=[
            pltpu.VMEM((docs, width), jnp.bfloat16),
            pltpu.VMEM((docs, 128), jnp.bfloat16),
            pltpu.VMEM((docs, 128), jnp.float32),
            pltpu.VMEM((docs // 8, 128), jnp.float32),
            pltpu.VMEM((8, docs), jnp.float32),
            pltpu.VMEM((docs // 8, 128), jnp.float32),
        ],
        compiler_params=params,
        name="score",
    )(got.reshape(groups, units, 8, 128))
    returned = lax.all_to_all(
        best.reshape(devices, 1, 128), ("grp", "blk"), split_axis=0, concat_axis=0, tiled=True
    ).reshape(devices, 128)
    picked = pl.pallas_call(
        pick_kernel,
        out_shape=jax.ShapeDtypeStruct((1, rows), jnp.float32),
        compiler_params=params,
        name="pick",
    )(returned, label_row, lane_row)
    return picked.reshape(rows)


def solution(mesh):
    placed = (P(("grp", "blk"), None), P(("grp", "blk"), None), P(("grp", "blk")))
    return jax.shard_map(
        shards, mesh=mesh, in_specs=placed, out_specs=P(("grp", "blk")), check_vma=False
    )
```

```python
import jax
import jax.numpy as jnp
from jax import lax
from jax.experimental import pallas as pl
from jax.experimental.pallas import tpu as pltpu
from jax.sharding import PartitionSpec as P

MAIN = 8
TAIL = 4
CAP = MAIN + TAIL
GROUP = 4
TURNS = (0, 2, 1, 3)
NT = (((1,), (1,)), ((), ()))
VMEM_LIMIT = 48 * 1024 * 1024


def place_kernel(
    rows_hbm, label_hbm, order_hbm, out_ref, lane_ref, label_ref,
    rows, order_ref, unit, pick, members, marks, places, sems,
):
    count, width = rows.shape
    groups = out_ref.shape[0]
    devices = groups * GROUP
    half = width // 2
    main_rows, tail_rows = devices * MAIN, devices * TAIL
    parts = 4
    part_rows = count // parts
    copies = [
        pltpu.make_async_copy(source, target, sems.at[parts + k])
        for k, (source, target) in enumerate(((label_hbm, label_ref), (order_hbm, order_ref)))
    ]
    large = []
    for k in range(parts):
        at = pl.ds(k * part_rows, part_rows)
        large.append(pltpu.make_async_copy(rows_hbm.at[at, :], rows.at[at, :], sems.at[k]))
    for copy in copies + large:
        copy.start()
    for copy in copies:
        copy.wait()

    me = lax.axis_index("blk")
    labels = label_ref[...]
    carry = jnp.zeros((devices, 128), jnp.float32)
    inner = lax.broadcasted_iota(jnp.int32, (128, 256), 0)
    outer = lax.broadcasted_iota(jnp.int32, (128, 256), 1)
    before = ((inner < outer) | (outer >= 128)).astype(jnp.bfloat16)
    slot_of = lax.broadcasted_iota(jnp.int32, (128, 128), 0) >> 2
    digit_of = lax.broadcasted_iota(jnp.int32, (128, 128), 0) & 3
    shift = jnp.where(
        digit_of == 0, 12, jnp.where(digit_of == 1, 6, jnp.where(digit_of == 2, 0, 18))
    )
    positions = []
    for block in range(count // 128):
        at = slice(block * 128, (block + 1) * 128)
        part = labels[:, at]
        member = lax.broadcasted_iota(jnp.int32, (devices, 128), 0) == part
        ones = member.astype(jnp.float32).astype(jnp.bfloat16)
        members[:, at] = ones
        sums = jnp.dot(ones, before, preferred_element_type=jnp.float32)
        rank = jnp.where(member, sums[:, :128] + carry, 0.0)
        carry = carry + sums[:, 128:]
        position = jnp.sum(rank, axis=0, keepdims=True).astype(jnp.int32)
        positions.append(position)
        turned = (position + 2 * ((me - part) & 3)) & 7
        lane_ref[:, at] = jnp.where(position < MAIN, turned, MAIN + turned)
        digit = ((order_ref[:, at] + 262144) >> shift) & 63
        marks[:, at] = (
            jnp.where(slot_of == position, digit, 0).astype(jnp.float32).astype(jnp.bfloat16)
        )
    for copy in large:
        copy.wait()

    position = jnp.concatenate(positions, axis=1)
    index = lax.broadcasted_iota(jnp.int32, (128, 128), 0).astype(jnp.float32)
    index = jnp.concatenate([index.astype(jnp.bfloat16)] * (count // 128), axis=1)
    index = index.reshape(8, 16, count)
    one, zero = jnp.ones((), jnp.bfloat16), jnp.zeros((), jnp.bfloat16)

    def choose(first, chosen, code):
        code = jnp.where(chosen, code, -1).astype(jnp.float32)
        code = jnp.broadcast_to(code, (16, count)).astype(jnp.bfloat16)
        pick[first : first + 128, :] = jnp.where(index == code[None], one, zero).reshape(
            128, count
        )

    for block in range(main_rows // 128):
        choose(
            block * 128,
            ((labels >> 4) == block) & (position < MAIN),
            (labels & 15) * MAIN + position,
        )
    for block in range(tail_rows // 128):
        choose(
            main_rows + block * 128,
            ((labels >> 5) == block) & (position >= MAIN),
            (labels & 31) * TAIL + position - MAIN,
        )
    places[...] = lax.dot_general(
        members[...], marks[...], NT, preferred_element_type=jnp.float32
    )

    for k in range(parts):
        at = slice(k * part_rows, (k + 1) * part_rows)
        values = rows[at, :].astype(jnp.float32)
        scale = lax.rsqrt(
            jnp.mean(values * values, axis=1, keepdims=True) + 1e-06
        ) * width ** (-0.5)
        unit[at, :] = (values * scale).astype(jnp.bfloat16)

    turn = lax.broadcasted_iota(jnp.int32, (8, 128), 0) >> 1

    def put(tile, values):
        values = values.reshape(groups, GROUP, 8, 128)
        if tile:
            for e in range(GROUP):
                out_ref[:, CAP * e + tile] = values[:, e].astype(jnp.bfloat16)
            return
        for group in range(groups):
            out_ref[group, 0] = values[group, 0].astype(jnp.bfloat16)
            for e in range(1, GROUP + 1):
                at = group * GROUP + e - 1
                mixed = jnp.where(
                    turn == e - 1,
                    jnp.broadcast_to(places[at : at + 1, :], (8, 128)),
                    values[group, e - 1],
                )
                if e < GROUP:
                    mixed = jnp.where(turn >= e, values[group, e], mixed)
                out_ref[group, CAP * e] = mixed.astype(jnp.bfloat16)

    step = 256
    upper = lax.broadcasted_iota(jnp.int32, (devices // 2, 8, step), 1) >= 4
    for n in range(half // step):
        ends = (n * step, half + n * step)
        for first in ends:
            main = jnp.dot(
                pick[:main_rows, :],
                unit[:, first : first + step],
                preferred_element_type=jnp.float32,
            )
            for k in range(step // 128):
                put(first // 128 + k, main[:, k * 128 : (k + 1) * 128])
        low, high = (
            jnp.dot(
                pick[main_rows:, :],
                unit[:, first : first + step],
                preferred_element_type=jnp.float32,
            ).reshape(devices // 2, 8, step)
            for first in ends
        )
        folded = jnp.stack(
            [
                jnp.where(upper, pltpu.roll(high, 4, 1), low),
                jnp.where(upper, high, pltpu.roll(low, 4, 1)),
            ],
            axis=1,
        ).reshape(devices, 8, step)
        for k in range(step // 128):
            put(MAIN + n * step // 128 + k, folded[:, :, k * 128 : (k + 1) * 128])


def score_kernel(
    got_ref, best_ref, member, digits, column, row_best, col_best, results, ordered
):
    groups = got_ref.shape[0]
    devices = groups * GROUP
    docs, width = member.shape
    pieces = width // 128
    main_rows = devices * MAIN
    last = GROUP * CAP
    me = lax.axis_index("blk")
    line = lax.broadcasted_iota(jnp.int32, (8, 128), 0)
    lane = lax.broadcasted_iota(jnp.int32, (8, 128), 1)
    turn, owner = line >> 1, lane >> 2
    inner = (turn == 1) | (turn == 2)
    first_half = turn < 2

    def both(a, b):
        return jnp.concatenate([a, b], axis=0).astype(jnp.bfloat16)

    for group in range(groups):
        chunks = []
        for turns in range(GROUP):
            source = (me + turns) & 3
            base = CAP * source - jnp.where(source < me, 1, 0)
            tiles = [
                got_ref[group, jnp.clip(base + t, 0, last)].astype(jnp.float32)
                for t in range(CAP + 2)
            ]
            if turns:
                tiles = [
                    jnp.where(turn >= turns, tiles[t], tiles[t + 1]) for t in range(CAP + 1)
                ]
            tiles[0] = jnp.where(((turn - turns) & 3) >= me, tiles[0], tiles[CAP])
            chunks.append(tiles)
        places = got_ref[group, last].astype(jnp.float32)
        for e in range(GROUP - 1):
            places = jnp.where(
                turn == e, got_ref[group, CAP * (e + 1)].astype(jnp.float32), places
            )
        places = pltpu.roll(places, (8 - 2 * me) & 7, 0)
        places = [
            jnp.broadcast_to(places[2 * turns : 2 * turns + 1, :], (8, 128))
            for turns in range(GROUP)
        ]
        for k in range(2):
            a, b = TURNS[2 * k], TURNS[2 * k + 1]
            at = slice(group * 32 + k * 16, group * 32 + k * 16 + 16)
            for t in range(pieces):
                member[at, t * 128 : (t + 1) * 128] = both(chunks[a][t], chunks[b][t])
            digits[at, :] = both(
                *(
                    jnp.where(owner == ((line - 2 * turns) & 7), places[turns], 0.0)
                    for turns in (a, b)
                )
            )
        at = slice(main_rows + group * 16, main_rows + group * 16 + 16)
        for t in range(pieces // 2):
            a, b, c, d = (chunks[turns][MAIN + t] for turns in range(GROUP))
            member[at, t * 128 : (t + 1) * 128] = both(
                jnp.where(first_half, a, c), jnp.where(inner, b, d)
            )
            t = t + pieces // 2
            member[at, t * 128 : (t + 1) * 128] = both(
                pltpu.roll(jnp.where(first_half, c, a), 4, 0),
                pltpu.roll(jnp.where(inner, d, b), 4, 0),
            )
        digits[at, :] = both(
            jnp.where(
                owner == MAIN + (line & 3), jnp.where(first_half, places[0], places[2]), 0.0
            ),
            jnp.where(
                owner == MAIN + ((line - 2) & 3), jnp.where(inner, places[1], places[3]), 0.0
            ),
        )

    def weights(shape, axis):
        at = lax.broadcasted_iota(jnp.int32, shape, axis)
        digit = at & 3
        weight = jnp.where(
            digit == 0,
            4096.0,
            jnp.where(digit == 1, 64.0, jnp.where(digit == 2, 1.0, -262144.0)),
        )
        return jnp.where(at < 4 * CAP, weight, 0.0).astype(jnp.bfloat16)

    column[...] = jnp.dot(
        digits[...], weights((128, 128), 0), preferred_element_type=jnp.float32
    )
    place_row = lax.dot_general(
        weights((8, 128), 1), digits[...], NT, preferred_element_type=jnp.float32
    )
    step = 256
    col_best[...] = jnp.full_like(col_best, -1.0)
    for i in range(docs // step):
        mine = slice(i * step, (i + 1) * step)
        best = jnp.full((step, 128), -1.0, jnp.float32)
        for j in range(i + 1):
            theirs = slice(j * step, (j + 1) * step)
            scores = lax.dot_general(
                member[mine, :], member[theirs, :], NT, preferred_element_type=jnp.float32
            )
            for k in range(step // 128):
                at = j * step + k * 128
                part = scores[:, k * 128 : (k + 1) * 128]
                earlier = place_row[0:1, at : at + 128] < column[mine, :]
                best = jnp.maximum(best, jnp.where(earlier, part, -1.0))
                if j != i:
                    other = jnp.where(earlier, -1.0, part)
                    col_best[:, at : at + 128] = jnp.maximum(
                        col_best[:, at : at + 128],
                        jnp.max(other.reshape(step // 8, 8, 128), axis=0),
                    )
        best = jnp.broadcast_to(jnp.max(best, axis=1, keepdims=True), (step, 128))
        place = lax.broadcasted_iota(jnp.int32, (step, 128), 0) & 7
        if i * step >= main_rows:
            place = place + MAIN
        best = jnp.where(lax.broadcasted_iota(jnp.int32, (step, 128), 1) == place, best, -2.0)
        row_best[i * step // 8 : (i + 1) * step // 8, :] = jnp.max(
            best.reshape(step // 8, 8, 128), axis=1
        )

    own = (
        lax.broadcasted_iota(jnp.int32, (16, 128), 1) >> 3
        == lax.broadcasted_iota(jnp.int32, (16, 128), 0)
    )
    for block in range(docs // 128):
        best = jnp.max(col_best[:, block * 128 : (block + 1) * 128], axis=0, keepdims=True)
        best = jnp.where(own, jnp.broadcast_to(best, (16, 128)), -2.0)
        for shift in (64, 32, 16, 8):
            best = jnp.maximum(best, pltpu.roll(best, shift, 1))
        at = slice(block * 16, (block + 1) * 16)
        results[at, :] = jnp.maximum(best, row_best[at, :])
    lane = lax.broadcasted_iota(jnp.int32, (groups, 128), 1)
    for index, turns in enumerate(TURNS):
        best = jnp.where(
            lane < MAIN,
            results[pl.ds(index, groups, stride=GROUP), :],
            results[pl.ds(devices + index // 2, groups, stride=2), :],
        )
        for e in range(GROUP):

            @pl.when(me == e)
            def _():
                ordered[pl.ds((e + turns) % GROUP, groups, stride=GROUP), :] = best

    best_ref[...] = ordered[:devices, :]


def pick_kernel(got_ref, label_ref, lane_ref, out_ref):
    devices = got_ref.shape[0]
    count = label_ref.shape[1]
    table = got_ref[...].T[: 2 * MAIN, :]
    top = table.astype(jnp.bfloat16).astype(jnp.float32)
    rest = table - top
    middle = rest.astype(jnp.bfloat16).astype(jnp.float32)
    parts = jnp.concatenate([top, middle, rest - middle], axis=0).astype(jnp.bfloat16)
    chosen = lax.broadcasted_iota(jnp.int32, (devices, count), 0) == label_ref[...]
    values = jnp.dot(
        parts,
        chosen.astype(jnp.float32).astype(jnp.bfloat16),
        preferred_element_type=jnp.float32,
    )
    values = (values[: 2 * MAIN] + values[2 * MAIN : 4 * MAIN]) + values[4 * MAIN :]
    line = lax.broadcasted_iota(jnp.int32, (2 * MAIN, count), 0)
    out_ref[...] = jnp.sum(
        jnp.where(line == lane_ref[...], values, 0.0), axis=0, keepdims=True
    )


def shards(embeddings, labels, order_ids):
    rows, width = embeddings.shape
    devices = lax.axis_size("grp") * lax.axis_size("blk")
    groups, units = devices // GROUP, GROUP * CAP + 1
    docs = devices * CAP
    params = pltpu.CompilerParams(vmem_limit_bytes=VMEM_LIMIT)
    in_hbm = pl.BlockSpec(memory_space=pltpu.HBM)
    outgoing, lane_row, label_row = pl.pallas_call(
        place_kernel,
        in_specs=[in_hbm] * 3,
        out_shape=[
            jax.ShapeDtypeStruct((groups, units, 8, 128), jnp.bfloat16),
            jax.ShapeDtypeStruct((1, rows), jnp.int32),
            jax.ShapeDtypeStruct((1, rows), jnp.int32),
        ],
        scratch_shapes=[
            pltpu.VMEM((rows, width), jnp.bfloat16),
            pltpu.VMEM((1, rows), jnp.int32),
            pltpu.VMEM((rows, width), jnp.bfloat16),
            pltpu.VMEM((docs, rows), jnp.bfloat16),
            pltpu.VMEM((devices, rows), jnp.bfloat16),
            pltpu.VMEM((128, rows), jnp.bfloat16),
            pltpu.VMEM((devices, 128), jnp.float32),
            pltpu.SemaphoreType.DMA((6,)),
        ],
        compiler_params=params,
        name="place",
    )(
        *(
            pltpu.with_memory_space_constraint(x, pltpu.HBM)
            for x in (embeddings, labels.reshape(1, rows), order_ids.reshape(1, rows))
        )
    )
    got = lax.all_to_all(
        outgoing.reshape(devices, units, 2, 128),
        ("grp", "blk"),
        split_axis=0,
        concat_axis=0,
        tiled=True,
    )
    best = pl.pallas_call(
        score_kernel,
        out_shape=jax.ShapeDtypeStruct((devices, 128), jnp.float32),
        scratch_shapes=[
            pltpu.VMEM((docs, width), jnp.bfloat16),
            pltpu.VMEM((docs, 128), jnp.bfloat16),
            pltpu.VMEM((docs, 128), jnp.float32),
            pltpu.VMEM((docs // 8, 128), jnp.float32),
            pltpu.VMEM((8, docs), jnp.float32),
            pltpu.VMEM((docs // 8 + 8, 128), jnp.float32),
            pltpu.VMEM((devices + 8, 128), jnp.float32),
        ],
        compiler_params=params,
        name="score",
    )(got.reshape(groups, units, 8, 128))
    returned = lax.all_to_all(
        best.reshape(devices, 1, 128), ("grp", "blk"), split_axis=0, concat_axis=0, tiled=True
    ).reshape(devices, 128)
    picked = pl.pallas_call(
        pick_kernel,
        out_shape=jax.ShapeDtypeStruct((1, rows), jnp.float32),
        compiler_params=params,
        name="pick",
    )(returned, label_row, lane_row)
    return picked.reshape(rows)


def solution(mesh):
    placed = (P(("grp", "blk"), None), P(("grp", "blk"), None), P(("grp", "blk")))
    return jax.shard_map(
        shards, mesh=mesh, in_specs=placed, out_specs=P(("grp", "blk")), check_vma=False
    )
```

```python
import jax
import jax.numpy as jnp
from jax import lax
from jax.experimental import pallas as pl
from jax.experimental.pallas import tpu as pltpu
from jax.sharding import PartitionSpec as P

MAIN = 8
TAIL = 4
CAP = MAIN + TAIL
GROUP = 4
TURNS = (0, 2, 1, 3)
NT = (((1,), (1,)), ((), ()))
VMEM_LIMIT = 48 * 1024 * 1024


def place_kernel(
    rows_hbm, label_hbm, order_hbm, out_ref, lane_ref, label_ref,
    rows, order_ref, pick, tail_pick, members, marks, places, sems, *unit,
):
    count, width = rows.shape
    groups = out_ref.shape[0]
    devices = groups * GROUP
    half = width // 2
    main_rows, tail_rows = devices * MAIN, devices * TAIL
    step = unit[0].shape[1]
    parts = 4
    part_rows = count // parts
    copies = [
        pltpu.make_async_copy(source, target, sems.at[parts + k])
        for k, (source, target) in enumerate(((label_hbm, label_ref), (order_hbm, order_ref)))
    ]
    large = []
    for k in range(parts):
        at = pl.ds(k * part_rows, part_rows)
        large.append(pltpu.make_async_copy(rows_hbm.at[at, :], rows.at[at, :], sems.at[k]))
    for copy in copies + large:
        copy.start()
    for copy in copies:
        copy.wait()

    me = lax.axis_index("blk")
    labels = label_ref[...]
    carry = jnp.zeros((devices, 128), jnp.float32)
    inner = lax.broadcasted_iota(jnp.int32, (128, 256), 0)
    outer = lax.broadcasted_iota(jnp.int32, (128, 256), 1)
    before = ((inner < outer) | (outer >= 128)).astype(jnp.bfloat16)
    slot_of = lax.broadcasted_iota(jnp.int32, (128, 128), 0) >> 2
    digit_of = lax.broadcasted_iota(jnp.int32, (128, 128), 0) & 3
    shift = jnp.where(
        digit_of == 0, 12, jnp.where(digit_of == 1, 6, jnp.where(digit_of == 2, 0, 18))
    )
    positions = []
    for block in range(count // 128):
        at = slice(block * 128, (block + 1) * 128)
        part = labels[:, at]
        member = lax.broadcasted_iota(jnp.int32, (devices, 128), 0) == part
        ones = member.astype(jnp.float32).astype(jnp.bfloat16)
        members[:, at] = ones
        sums = jnp.dot(ones, before, preferred_element_type=jnp.float32)
        rank = jnp.where(member, sums[:, :128] + carry, 0.0)
        carry = carry + sums[:, 128:]
        position = jnp.sum(rank, axis=0, keepdims=True).astype(jnp.int32)
        positions.append(position)
        turned = (position + 2 * ((me - part) & 3)) & 7
        lane_ref[:, at] = jnp.where(position < MAIN, turned, MAIN + turned)
        digit = ((order_ref[:, at] + 262144) >> shift) & 63
        marks[:, at] = (
            jnp.where(slot_of == position, digit, 0).astype(jnp.float32).astype(jnp.bfloat16)
        )
    for copy in large:
        copy.wait()

    position = jnp.concatenate(positions, axis=1)
    index = lax.broadcasted_iota(jnp.int32, (128, 128), 0).astype(jnp.float32)
    index = jnp.concatenate([index.astype(jnp.bfloat16)] * (count // 128), axis=1)
    index = index.reshape(8, 16, count)
    one, zero = jnp.ones((), jnp.bfloat16), jnp.zeros((), jnp.bfloat16)

    def choose(pick, first, chosen, code):
        code = jnp.where(chosen, code, -1).astype(jnp.float32)
        code = jnp.broadcast_to(code, (16, count)).astype(jnp.bfloat16)
        pick[first : first + 128, :] = jnp.where(index == code[None], one, zero).reshape(
            128, count
        )

    for block in range(main_rows // 128):
        choose(
            pick,
            block * 128,
            ((labels >> 4) == block) & (position < MAIN),
            (labels & 15) * MAIN + position,
        )
    for block in range(tail_rows // 128):
        choose(
            tail_pick,
            block * 128,
            ((labels >> 5) == block) & (position >= MAIN),
            (labels & 31) * TAIL + position - MAIN,
        )
    places[...] = lax.dot_general(
        members[...], marks[...], NT, preferred_element_type=jnp.float32
    )

    for k in range(parts):
        at = slice(k * part_rows, (k + 1) * part_rows)
        values = rows[at, :].astype(jnp.float32)
        scale = lax.rsqrt(
            jnp.mean(values * values, axis=1, keepdims=True) + 1e-06
        ) * width ** (-0.5)
        values = (values * scale).astype(jnp.bfloat16)
        for n, columns in enumerate(unit):
            columns[at, :] = values[:, n * step : (n + 1) * step]

    turn = lax.broadcasted_iota(jnp.int32, (8, 128), 0) >> 1

    def put(tile, values):
        values = values.reshape(groups, GROUP, 8, 128)
        if tile:
            for e in range(GROUP):
                out_ref[:, CAP * e + tile] = values[:, e].astype(jnp.bfloat16)
            return
        for group in range(groups):
            out_ref[group, 0] = values[group, 0].astype(jnp.bfloat16)
            for e in range(1, GROUP + 1):
                at = group * GROUP + e - 1
                mixed = jnp.where(
                    turn == e - 1,
                    jnp.broadcast_to(places[at : at + 1, :], (8, 128)),
                    values[group, e - 1],
                )
                if e < GROUP:
                    mixed = jnp.where(turn >= e, values[group, e], mixed)
                out_ref[group, CAP * e] = mixed.astype(jnp.bfloat16)

    upper = lax.broadcasted_iota(jnp.int32, (devices // 2, 8, step), 1) >= 4
    for n in range(half // step):
        ends = (n * step, half + n * step)
        for first in ends:
            main = jnp.dot(
                pick[...],
                unit[first // step][...],
                preferred_element_type=jnp.float32,
            )
            for k in range(step // 128):
                put(first // 128 + k, main[:, k * 128 : (k + 1) * 128])
        low, high = (
            jnp.dot(
                tail_pick[...],
                unit[first // step][...],
                preferred_element_type=jnp.float32,
            ).reshape(devices // 2, 8, step)
            for first in ends
        )
        folded = jnp.stack(
            [
                jnp.where(upper, pltpu.roll(high, 4, 1), low),
                jnp.where(upper, high, pltpu.roll(low, 4, 1)),
            ],
            axis=1,
        ).reshape(devices, 8, step)
        for k in range(step // 128):
            put(MAIN + n * step // 128 + k, folded[:, :, k * 128 : (k + 1) * 128])


def score_kernel(
    got_ref, best_ref, digits, column, row_best, results, ordered, *member
):
    groups = got_ref.shape[0]
    devices = groups * GROUP
    step, width = member[0].shape
    docs = step * len(member)
    pieces = width // 128
    main_rows = devices * MAIN
    last = GROUP * CAP
    me = lax.axis_index("blk")
    line = lax.broadcasted_iota(jnp.int32, (8, 128), 0)
    lane = lax.broadcasted_iota(jnp.int32, (8, 128), 1)
    turn, owner = line >> 1, lane >> 2
    inner = (turn == 1) | (turn == 2)
    first_half = turn < 2

    def both(a, b):
        return jnp.concatenate([a, b], axis=0).astype(jnp.bfloat16)

    def put(first, t, values):
        at = slice(first % step, first % step + 16)
        member[first // step][at, t * 128 : (t + 1) * 128] = values

    for group in range(groups):
        chunks = []
        for turns in range(GROUP):
            source = (me + turns) & 3
            base = CAP * source - jnp.where(source < me, 1, 0)
            tiles = [
                got_ref[group, jnp.clip(base + t, 0, last)].astype(jnp.float32)
                for t in range(CAP + 2)
            ]
            if turns:
                tiles = [
                    jnp.where(turn >= turns, tiles[t], tiles[t + 1]) for t in range(CAP + 1)
                ]
            tiles[0] = jnp.where(((turn - turns) & 3) >= me, tiles[0], tiles[CAP])
            chunks.append(tiles)
        places = got_ref[group, last].astype(jnp.float32)
        for e in range(GROUP - 1):
            places = jnp.where(
                turn == e, got_ref[group, CAP * (e + 1)].astype(jnp.float32), places
            )
        places = pltpu.roll(places, (8 - 2 * me) & 7, 0)
        places = [
            jnp.broadcast_to(places[2 * turns : 2 * turns + 1, :], (8, 128))
            for turns in range(GROUP)
        ]
        for k in range(2):
            a, b = TURNS[2 * k], TURNS[2 * k + 1]
            at = slice(group * 32 + k * 16, group * 32 + k * 16 + 16)
            for t in range(pieces):
                put(at.start, t, both(chunks[a][t], chunks[b][t]))
            digits[at, :] = both(
                *(
                    jnp.where(owner == ((line - 2 * turns) & 7), places[turns], 0.0)
                    for turns in (a, b)
                )
            )
        at = slice(main_rows + group * 16, main_rows + group * 16 + 16)
        for t in range(pieces // 2):
            a, b, c, d = (chunks[turns][MAIN + t] for turns in range(GROUP))
            put(at.start, t, both(jnp.where(first_half, a, c), jnp.where(inner, b, d)))
            t = t + pieces // 2
            high = both(
                pltpu.roll(jnp.where(first_half, c, a), 4, 0),
                pltpu.roll(jnp.where(inner, d, b), 4, 0),
            )
            put(at.start, t, high)
        digits[at, :] = both(
            jnp.where(
                owner == MAIN + (line & 3), jnp.where(first_half, places[0], places[2]), 0.0
            ),
            jnp.where(
                owner == MAIN + ((line - 2) & 3), jnp.where(inner, places[1], places[3]), 0.0
            ),
        )

    def weights(shape, axis):
        at = lax.broadcasted_iota(jnp.int32, shape, axis)
        digit = at & 3
        weight = jnp.where(
            digit == 0,
            4096.0,
            jnp.where(digit == 1, 64.0, jnp.where(digit == 2, 1.0, -262144.0)),
        )
        return jnp.where(at < 4 * CAP, weight, 0.0).astype(jnp.bfloat16)

    column[...] = jnp.dot(
        digits[...], weights((128, 128), 0), preferred_element_type=jnp.float32
    )
    place_row = lax.dot_general(
        weights((8, 128), 1), digits[...], NT, preferred_element_type=jnp.float32
    )
    col_best = [jnp.full((8, 128), -1.0, jnp.float32)] * (docs // 128)
    for i in range(docs // step):
        mine = slice(i * step, (i + 1) * step)
        best = jnp.full((step, 128), -1.0, jnp.float32)
        for j in range(i + 1):
            scores = lax.dot_general(
                member[i][...], member[j][...], NT, preferred_element_type=jnp.float32
            )
            for k in range(step // 128):
                at = j * step + k * 128
                part = scores[:, k * 128 : (k + 1) * 128]
                earlier = place_row[0:1, at : at + 128] < column[mine, :]
                best = jnp.maximum(best, jnp.where(earlier, part, -1.0))
                if j != i:
                    other = jnp.where(earlier, -1.0, part)
                    col_best[at // 128] = jnp.maximum(
                        col_best[at // 128],
                        jnp.max(other.reshape(step // 8, 8, 128), axis=0),
                    )
        best = jnp.broadcast_to(jnp.max(best, axis=1, keepdims=True), (step, 128))
        place = lax.broadcasted_iota(jnp.int32, (step, 128), 0) & 7
        if i * step >= main_rows:
            place = place + MAIN
        best = jnp.where(lax.broadcasted_iota(jnp.int32, (step, 128), 1) == place, best, -2.0)
        row_best[i * step // 8 : (i + 1) * step // 8, :] = jnp.max(
            best.reshape(step // 8, 8, 128), axis=1
        )

    own = (
        lax.broadcasted_iota(jnp.int32, (16, 128), 1) >> 3
        == lax.broadcasted_iota(jnp.int32, (16, 128), 0)
    )
    for block in range(docs // 128):
        best = jnp.max(col_best[block], axis=0, keepdims=True)
        best = jnp.where(own, jnp.broadcast_to(best, (16, 128)), -2.0)
        for shift in (64, 32, 16, 8):
            best = jnp.maximum(best, pltpu.roll(best, shift, 1))
        at = slice(block * 16, (block + 1) * 16)
        results[at, :] = jnp.maximum(best, row_best[at, :])
    lane = lax.broadcasted_iota(jnp.int32, (groups, 128), 1)
    for index, turns in enumerate(TURNS):
        best = jnp.where(
            lane < MAIN,
            results[pl.ds(index, groups, stride=GROUP), :],
            results[pl.ds(devices + index // 2, groups, stride=2), :],
        )
        for e in range(GROUP):

            @pl.when(me == e)
            def _():
                ordered[pl.ds((e + turns) % GROUP, groups, stride=GROUP), :] = best

    best_ref[...] = ordered[:devices, :]


def pick_kernel(got_ref, label_ref, lane_ref, out_ref):
    devices = got_ref.shape[0]
    count = label_ref.shape[1]
    table = got_ref[...].T[: 2 * MAIN, :]
    top = table.astype(jnp.bfloat16).astype(jnp.float32)
    rest = table - top
    middle = rest.astype(jnp.bfloat16).astype(jnp.float32)
    parts = jnp.concatenate([top, middle, rest - middle], axis=0).astype(jnp.bfloat16)
    chosen = lax.broadcasted_iota(jnp.int32, (devices, count), 0) == label_ref[...]
    values = jnp.dot(
        parts,
        chosen.astype(jnp.float32).astype(jnp.bfloat16),
        preferred_element_type=jnp.float32,
    )
    values = (values[: 2 * MAIN] + values[2 * MAIN : 4 * MAIN]) + values[4 * MAIN :]
    line = lax.broadcasted_iota(jnp.int32, (2 * MAIN, count), 0)
    out_ref[...] = jnp.sum(
        jnp.where(line == lane_ref[...], values, 0.0), axis=0, keepdims=True
    )


def shards(embeddings, labels, order_ids):
    rows, width = embeddings.shape
    devices = lax.axis_size("grp") * lax.axis_size("blk")
    groups, units = devices // GROUP, GROUP * CAP + 1
    docs, step = devices * CAP, 256
    params = pltpu.CompilerParams(vmem_limit_bytes=VMEM_LIMIT)
    in_hbm = pl.BlockSpec(memory_space=pltpu.HBM)
    outgoing, lane_row, label_row = pl.pallas_call(
        place_kernel,
        in_specs=[in_hbm] * 3,
        out_shape=[
            jax.ShapeDtypeStruct((groups, units, 8, 128), jnp.bfloat16),
            jax.ShapeDtypeStruct((1, rows), jnp.int32),
            jax.ShapeDtypeStruct((1, rows), jnp.int32),
        ],
        scratch_shapes=[
            pltpu.VMEM((rows, width), jnp.bfloat16),
            pltpu.VMEM((1, rows), jnp.int32),
            pltpu.VMEM((devices * MAIN, rows), jnp.bfloat16),
            pltpu.VMEM((devices * TAIL, rows), jnp.bfloat16),
            pltpu.VMEM((devices, rows), jnp.bfloat16),
            pltpu.VMEM((128, rows), jnp.bfloat16),
            pltpu.VMEM((devices, 128), jnp.float32),
            pltpu.SemaphoreType.DMA((6,)),
        ]
        + [pltpu.VMEM((rows, step), jnp.bfloat16)] * (width // step),
        compiler_params=params,
        name="place",
    )(
        *(
            pltpu.with_memory_space_constraint(x, pltpu.HBM)
            for x in (embeddings, labels.reshape(1, rows), order_ids.reshape(1, rows))
        )
    )
    got = lax.all_to_all(
        outgoing.reshape(devices, units, 2, 128),
        ("grp", "blk"),
        split_axis=0,
        concat_axis=0,
        tiled=True,
    )
    best = pl.pallas_call(
        score_kernel,
        out_shape=jax.ShapeDtypeStruct((devices, 128), jnp.float32),
        scratch_shapes=[
            pltpu.VMEM((docs, 128), jnp.bfloat16),
            pltpu.VMEM((docs, 128), jnp.float32),
            pltpu.VMEM((docs // 8, 128), jnp.float32),
            pltpu.VMEM((docs // 8 + 8, 128), jnp.float32),
            pltpu.VMEM((devices + 8, 128), jnp.float32),
        ]
        + [pltpu.VMEM((step, width), jnp.bfloat16)] * (docs // step),
        compiler_params=params,
        name="score",
    )(got.reshape(groups, units, 8, 128))
    returned = lax.all_to_all(
        best.reshape(devices, 1, 128), ("grp", "blk"), split_axis=0, concat_axis=0, tiled=True
    ).reshape(devices, 128)
    picked = pl.pallas_call(
        pick_kernel,
        out_shape=jax.ShapeDtypeStruct((1, rows), jnp.float32),
        compiler_params=params,
        name="pick",
    )(returned, label_row, lane_row)
    return picked.reshape(rows)


def solution(mesh):
    placed = (P(("grp", "blk"), None), P(("grp", "blk"), None), P(("grp", "blk")))
    return jax.shard_map(
        shards, mesh=mesh, in_specs=placed, out_specs=P(("grp", "blk")), check_vma=False
    )
```

```python
import jax
import jax.numpy as jnp
from jax import lax
from jax.experimental import pallas as pl
from jax.experimental.pallas import tpu as pltpu
from jax.sharding import PartitionSpec as P

MAIN = 8
TAIL = 4
CAP = MAIN + TAIL
GROUP = 4
TURNS = (0, 2, 1, 3)
NT = (((1,), (1,)), ((), ()))
VMEM_LIMIT = 48 * 1024 * 1024


def place_kernel(
    rows_hbm, label_hbm, order_hbm, out_ref, lane_ref, label_ref,
    rows, order_ref, pick, tail_pick, members, marks, places, sems, *unit,
):
    count, width = rows.shape
    groups = out_ref.shape[0]
    devices = groups * GROUP
    half = width // 2
    main_rows, tail_rows = devices * MAIN, devices * TAIL
    step = unit[0].shape[1]
    parts = 4
    part_rows = count // parts
    copies = [
        pltpu.make_async_copy(source, target, sems.at[parts + k])
        for k, (source, target) in enumerate(((label_hbm, label_ref), (order_hbm, order_ref)))
    ]
    large = []
    for k in range(parts):
        at = pl.ds(k * part_rows, part_rows)
        large.append(pltpu.make_async_copy(rows_hbm.at[at, :], rows.at[at, :], sems.at[k]))
    for copy in copies + large:
        copy.start()
    for copy in copies:
        copy.wait()

    me = lax.axis_index("blk")
    labels = label_ref[...]
    carry = jnp.zeros((devices, 128), jnp.float32)
    inner = lax.broadcasted_iota(jnp.int32, (128, 256), 0)
    outer = lax.broadcasted_iota(jnp.int32, (128, 256), 1)
    before = ((inner < outer) | (outer >= 128)).astype(jnp.bfloat16)
    slot_of = lax.broadcasted_iota(jnp.int32, (128, 128), 0) >> 2
    digit_of = lax.broadcasted_iota(jnp.int32, (128, 128), 0) & 3
    shift = jnp.where(
        digit_of == 0, 12, jnp.where(digit_of == 1, 6, jnp.where(digit_of == 2, 0, 18))
    )
    positions = []
    for block in range(count // 128):
        at = slice(block * 128, (block + 1) * 128)
        part = labels[:, at]
        member = lax.broadcasted_iota(jnp.int32, (devices, 128), 0) == part
        ones = member.astype(jnp.float32).astype(jnp.bfloat16)
        members[:, at] = ones
        sums = jnp.dot(ones, before, preferred_element_type=jnp.float32)
        rank = jnp.where(member, sums[:, :128] + carry, 0.0)
        carry = carry + sums[:, 128:]
        position = jnp.sum(rank, axis=0, keepdims=True).astype(jnp.int32)
        positions.append(position)
        turned = (position + 2 * ((me - part) & 3)) & 7
        lane_ref[:, at] = jnp.where(position < MAIN, turned, MAIN + turned)
        digit = ((order_ref[:, at] + 262144) >> shift) & 63
        marks[:, at] = (
            jnp.where(slot_of == position, digit, 0).astype(jnp.float32).astype(jnp.bfloat16)
        )
    for copy in large:
        copy.wait()

    position = jnp.concatenate(positions, axis=1)
    index = lax.broadcasted_iota(jnp.int32, (128, 128), 0).astype(jnp.float32)
    index = jnp.concatenate([index.astype(jnp.bfloat16)] * (count // 128), axis=1)
    index = index.reshape(8, 16, count)
    one, zero = jnp.ones((), jnp.bfloat16), jnp.zeros((), jnp.bfloat16)

    def choose(pick, first, chosen, code):
        code = jnp.where(chosen, code, -1).astype(jnp.float32)
        code = jnp.broadcast_to(code, (16, count)).astype(jnp.bfloat16)
        pick[first : first + 128, :] = jnp.where(index == code[None], one, zero).reshape(
            128, count
        )

    for block in range(main_rows // 128):
        choose(
            pick,
            block * 128,
            ((labels >> 4) == block) & (position < MAIN),
            (labels & 15) * MAIN + position,
        )
    for block in range(tail_rows // 128):
        choose(
            tail_pick,
            block * 128,
            ((labels >> 5) == block) & (position >= MAIN),
            (labels & 31) * TAIL + position - MAIN,
        )
    places[...] = lax.dot_general(
        members[...], marks[...], NT, preferred_element_type=jnp.float32
    )

    for k in range(parts):
        at = slice(k * part_rows, (k + 1) * part_rows)
        values = rows[at, :].astype(jnp.float32)
        scale = lax.rsqrt(
            jnp.mean(values * values, axis=1, keepdims=True) + 1e-06
        ) * width ** (-0.5)
        values = (values * scale).astype(jnp.bfloat16)
        for n, columns in enumerate(unit):
            columns[at, :] = values[:, n * step : (n + 1) * step]

    turn = lax.broadcasted_iota(jnp.int32, (8, 128), 0) >> 1

    def put(tile, values):
        values = values.reshape(groups, GROUP, 8, 128)
        if tile:
            for e in range(GROUP):
                out_ref[:, CAP * e + tile] = values[:, e].astype(jnp.bfloat16)
            return
        for group in range(groups):
            out_ref[group, 0] = values[group, 0].astype(jnp.bfloat16)
            for e in range(1, GROUP + 1):
                at = group * GROUP + e - 1
                mixed = jnp.where(
                    turn == e - 1,
                    jnp.broadcast_to(places[at : at + 1, :], (8, 128)),
                    values[group, e - 1],
                )
                if e < GROUP:
                    mixed = jnp.where(turn >= e, values[group, e], mixed)
                out_ref[group, CAP * e] = mixed.astype(jnp.bfloat16)

    upper = lax.broadcasted_iota(jnp.int32, (devices // 2, 8, step), 1) >= 4
    for n in range(half // step):
        ends = (n * step, half + n * step)
        for first in ends:
            main = jnp.dot(
                pick[...],
                unit[first // step][...],
                preferred_element_type=jnp.float32,
            )
            for k in range(step // 128):
                put(first // 128 + k, main[:, k * 128 : (k + 1) * 128])
        low, high = (
            jnp.dot(
                tail_pick[...],
                unit[first // step][...],
                preferred_element_type=jnp.float32,
            ).reshape(devices // 2, 8, step)
            for first in ends
        )
        folded = jnp.stack(
            [
                jnp.where(upper, pltpu.roll(high, 4, 1), low),
                jnp.where(upper, high, pltpu.roll(low, 4, 1)),
            ],
            axis=1,
        ).reshape(devices, 8, step)
        for k in range(step // 128):
            put(MAIN + n * step // 128 + k, folded[:, :, k * 128 : (k + 1) * 128])


def score_kernel(
    got_ref, best_ref, digits, column, row_best, results, ordered, *member
):
    groups = got_ref.shape[0]
    devices = groups * GROUP
    step, width = member[0].shape
    docs = step * len(member)
    pieces = width // 128
    main_rows = devices * MAIN
    last = GROUP * CAP
    me = lax.axis_index("blk")
    line = lax.broadcasted_iota(jnp.int32, (8, 128), 0)
    lane = lax.broadcasted_iota(jnp.int32, (8, 128), 1)
    turn, owner = line >> 1, lane >> 2
    inner = (turn == 1) | (turn == 2)
    first_half = turn < 2

    def both(a, b):
        return jnp.concatenate([a, b], axis=0).astype(jnp.bfloat16)

    def put(first, t, values):
        at = slice(first % step, first % step + 16)
        member[first // step][at, t * 128 : (t + 1) * 128] = values

    for group in range(groups):
        chunks = []
        for turns in range(GROUP):
            source = (me + turns) & 3
            base = CAP * source - jnp.where(source < me, 1, 0)
            tiles = [
                got_ref[group, jnp.clip(base + t, 0, last)].astype(jnp.float32)
                for t in range(CAP + 2)
            ]
            if turns:
                tiles = [
                    jnp.where(turn >= turns, tiles[t], tiles[t + 1]) for t in range(CAP + 1)
                ]
            tiles[0] = jnp.where(((turn - turns) & 3) >= me, tiles[0], tiles[CAP])
            chunks.append(tiles)
        places = got_ref[group, last].astype(jnp.float32)
        for e in range(GROUP - 1):
            places = jnp.where(
                turn == e, got_ref[group, CAP * (e + 1)].astype(jnp.float32), places
            )
        places = pltpu.roll(places, (8 - 2 * me) & 7, 0)
        places = [
            jnp.broadcast_to(places[2 * turns : 2 * turns + 1, :], (8, 128))
            for turns in range(GROUP)
        ]
        for k in range(2):
            a, b = TURNS[2 * k], TURNS[2 * k + 1]
            at = slice(group * 32 + k * 16, group * 32 + k * 16 + 16)
            for t in range(pieces):
                put(at.start, t, both(chunks[a][t], chunks[b][t]))
            digits[at, :] = both(
                *(
                    jnp.where(owner == ((line - 2 * turns) & 7), places[turns], 0.0)
                    for turns in (a, b)
                )
            )
        at = slice(main_rows + group * 16, main_rows + group * 16 + 16)
        for t in range(pieces // 2):
            a, b, c, d = (chunks[turns][MAIN + t] for turns in range(GROUP))
            put(at.start, t, both(jnp.where(first_half, a, c), jnp.where(inner, b, d)))
            t = t + pieces // 2
            high = both(
                pltpu.roll(jnp.where(first_half, c, a), 4, 0),
                pltpu.roll(jnp.where(inner, d, b), 4, 0),
            )
            put(at.start, t, high)
        digits[at, :] = both(
            jnp.where(
                owner == MAIN + (line & 3), jnp.where(first_half, places[0], places[2]), 0.0
            ),
            jnp.where(
                owner == MAIN + ((line - 2) & 3), jnp.where(inner, places[1], places[3]), 0.0
            ),
        )

    def weights(shape, axis):
        at = lax.broadcasted_iota(jnp.int32, shape, axis)
        digit = at & 3
        weight = jnp.where(
            digit == 0,
            4096.0,
            jnp.where(digit == 1, 64.0, jnp.where(digit == 2, 1.0, -262144.0)),
        )
        return jnp.where(at < 4 * CAP, weight, 0.0).astype(jnp.bfloat16)

    column[...] = jnp.dot(
        digits[...], weights((128, 128), 0), preferred_element_type=jnp.float32
    )
    place_row = lax.dot_general(
        weights((8, 128), 1), digits[...], NT, preferred_element_type=jnp.float32
    )
    col_best = [jnp.full((8, 128), -1.0, jnp.float32)] * (docs // 128)
    for i in range(docs // step):
        mine = slice(i * step, (i + 1) * step)
        best = jnp.full((step, 128), -1.0, jnp.float32)
        half = step // 2

        def take(best, rows, scores, at, both_ways):
            earlier = place_row[0:1, at : at + 128] < column[rows, :]
            best = jnp.maximum(best, jnp.where(earlier, scores, -1.0))
            if both_ways:
                other = jnp.where(earlier, -1.0, scores).reshape(-1, 8, 128)
                col_best[at // 128] = jnp.maximum(col_best[at // 128], jnp.max(other, axis=0))
            return best

        for j in range(i):
            scores = lax.dot_general(
                member[i][...], member[j][...], NT, preferred_element_type=jnp.float32
            )
            for k in range(step // 128):
                part = scores[:, k * 128 : (k + 1) * 128]
                best = take(best, mine, part, j * step + k * 128, True)
        low = lax.dot_general(
            member[i][half:, :], member[i][...], NT, preferred_element_type=jnp.float32
        )
        high = lax.dot_general(
            member[i][:half, :], member[i][:half, :], NT, preferred_element_type=jnp.float32
        )
        first = i * step
        top = take(best[:half], slice(first, first + half), high, first, False)
        rows = slice(first + half, first + step)
        bottom = take(best[half:], rows, low[:, :half], first, True)
        bottom = take(bottom, rows, low[:, half:], first + half, False)
        best = jnp.concatenate([top, bottom], axis=0)
        best = jnp.broadcast_to(jnp.max(best, axis=1, keepdims=True), (step, 128))
        place = lax.broadcasted_iota(jnp.int32, (step, 128), 0) & 7
        if i * step >= main_rows:
            place = place + MAIN
        best = jnp.where(lax.broadcasted_iota(jnp.int32, (step, 128), 1) == place, best, -2.0)
        row_best[i * step // 8 : (i + 1) * step // 8, :] = jnp.max(
            best.reshape(step // 8, 8, 128), axis=1
        )

    own = (
        lax.broadcasted_iota(jnp.int32, (16, 128), 1) >> 3
        == lax.broadcasted_iota(jnp.int32, (16, 128), 0)
    )
    for block in range(docs // 128):
        best = jnp.max(col_best[block], axis=0, keepdims=True)
        best = jnp.where(own, jnp.broadcast_to(best, (16, 128)), -2.0)
        for shift in (64, 32, 16, 8):
            best = jnp.maximum(best, pltpu.roll(best, shift, 1))
        at = slice(block * 16, (block + 1) * 16)
        results[at, :] = jnp.maximum(best, row_best[at, :])
    lane = lax.broadcasted_iota(jnp.int32, (groups, 128), 1)
    for index, turns in enumerate(TURNS):
        best = jnp.where(
            lane < MAIN,
            results[pl.ds(index, groups, stride=GROUP), :],
            results[pl.ds(devices + index // 2, groups, stride=2), :],
        )
        for e in range(GROUP):

            @pl.when(me == e)
            def _():
                ordered[pl.ds((e + turns) % GROUP, groups, stride=GROUP), :] = best

    best_ref[...] = ordered[:devices, :]


def pick_kernel(got_ref, label_ref, lane_ref, out_ref):
    devices = got_ref.shape[0]
    count = label_ref.shape[1]
    table = got_ref[...].T[: 2 * MAIN, :]
    top = table.astype(jnp.bfloat16).astype(jnp.float32)
    rest = table - top
    middle = rest.astype(jnp.bfloat16).astype(jnp.float32)
    parts = jnp.concatenate([top, middle, rest - middle], axis=0).astype(jnp.bfloat16)
    chosen = lax.broadcasted_iota(jnp.int32, (devices, count), 0) == label_ref[...]
    values = jnp.dot(
        parts,
        chosen.astype(jnp.float32).astype(jnp.bfloat16),
        preferred_element_type=jnp.float32,
    )
    values = (values[: 2 * MAIN] + values[2 * MAIN : 4 * MAIN]) + values[4 * MAIN :]
    line = lax.broadcasted_iota(jnp.int32, (2 * MAIN, count), 0)
    out_ref[...] = jnp.sum(
        jnp.where(line == lane_ref[...], values, 0.0), axis=0, keepdims=True
    )


def shards(embeddings, labels, order_ids):
    rows, width = embeddings.shape
    devices = lax.axis_size("grp") * lax.axis_size("blk")
    groups, units = devices // GROUP, GROUP * CAP + 1
    docs, step = devices * CAP, 256
    params = pltpu.CompilerParams(vmem_limit_bytes=VMEM_LIMIT)
    in_hbm = pl.BlockSpec(memory_space=pltpu.HBM)
    outgoing, lane_row, label_row = pl.pallas_call(
        place_kernel,
        in_specs=[in_hbm] * 3,
        out_shape=[
            jax.ShapeDtypeStruct((groups, units, 8, 128), jnp.bfloat16),
            jax.ShapeDtypeStruct((1, rows), jnp.int32),
            jax.ShapeDtypeStruct((1, rows), jnp.int32),
        ],
        scratch_shapes=[
            pltpu.VMEM((rows, width), jnp.bfloat16),
            pltpu.VMEM((1, rows), jnp.int32),
            pltpu.VMEM((devices * MAIN, rows), jnp.bfloat16),
            pltpu.VMEM((devices * TAIL, rows), jnp.bfloat16),
            pltpu.VMEM((devices, rows), jnp.bfloat16),
            pltpu.VMEM((128, rows), jnp.bfloat16),
            pltpu.VMEM((devices, 128), jnp.float32),
            pltpu.SemaphoreType.DMA((6,)),
        ]
        + [pltpu.VMEM((rows, step), jnp.bfloat16)] * (width // step),
        compiler_params=params,
        name="place",
    )(
        *(
            pltpu.with_memory_space_constraint(x, pltpu.HBM)
            for x in (embeddings, labels.reshape(1, rows), order_ids.reshape(1, rows))
        )
    )
    got = lax.all_to_all(
        outgoing.reshape(devices, units, 2, 128),
        ("grp", "blk"),
        split_axis=0,
        concat_axis=0,
        tiled=True,
    )
    best = pl.pallas_call(
        score_kernel,
        out_shape=jax.ShapeDtypeStruct((devices, 128), jnp.float32),
        scratch_shapes=[
            pltpu.VMEM((docs, 128), jnp.bfloat16),
            pltpu.VMEM((docs, 128), jnp.float32),
            pltpu.VMEM((docs // 8, 128), jnp.float32),
            pltpu.VMEM((docs // 8 + 8, 128), jnp.float32),
            pltpu.VMEM((devices + 8, 128), jnp.float32),
        ]
        + [pltpu.VMEM((step, width), jnp.bfloat16)] * (docs // step),
        compiler_params=params,
        name="score",
    )(got.reshape(groups, units, 8, 128))
    returned = lax.all_to_all(
        best.reshape(devices, 1, 128), ("grp", "blk"), split_axis=0, concat_axis=0, tiled=True
    ).reshape(devices, 128)
    picked = pl.pallas_call(
        pick_kernel,
        out_shape=jax.ShapeDtypeStruct((1, rows), jnp.float32),
        compiler_params=params,
        name="pick",
    )(returned, label_row, lane_row)
    return picked.reshape(rows)


def solution(mesh):
    placed = (P(("grp", "blk"), None), P(("grp", "blk"), None), P(("grp", "blk")))
    return jax.shard_map(
        shards, mesh=mesh, in_specs=placed, out_specs=P(("grp", "blk")), check_vma=False
    )
```

```python
import jax
import jax.numpy as jnp
from jax import lax
from jax.experimental import pallas as pl
from jax.experimental.pallas import tpu as pltpu
from jax.sharding import PartitionSpec as P

MAIN = 8
TAIL = 4
CAP = MAIN + TAIL
GROUP = 4
TURNS = (0, 2, 1, 3)
NT = (((1,), (1,)), ((), ()))
VMEM_LIMIT = 48 * 1024 * 1024


def place_kernel(
    rows_hbm, label_hbm, order_hbm, out_ref, lane_ref, label_ref,
    rows, order_ref, pick, tail_pick, members, marks, places, sems, *unit,
):
    count, width = rows.shape
    groups = out_ref.shape[0]
    devices = groups * GROUP
    half = width // 2
    main_rows, tail_rows = devices * MAIN, devices * TAIL
    step = unit[0].shape[1]
    parts = 4
    part_rows = count // parts
    copies = [
        pltpu.make_async_copy(source, target, sems.at[parts + k])
        for k, (source, target) in enumerate(((label_hbm, label_ref), (order_hbm, order_ref)))
    ]
    large = []
    for k in range(parts):
        at = pl.ds(k * part_rows, part_rows)
        large.append(pltpu.make_async_copy(rows_hbm.at[at, :], rows.at[at, :], sems.at[k]))
    for copy in copies + large:
        copy.start()
    for copy in copies:
        copy.wait()

    me = lax.axis_index("blk")
    labels = label_ref[...]
    carry = jnp.zeros((devices, 128), jnp.float32)
    inner = lax.broadcasted_iota(jnp.int32, (128, 256), 0)
    outer = lax.broadcasted_iota(jnp.int32, (128, 256), 1)
    before = ((inner < outer) | (outer >= 128)).astype(jnp.bfloat16)
    slot_of = lax.broadcasted_iota(jnp.int32, (128, 128), 0) >> 2
    digit_of = lax.broadcasted_iota(jnp.int32, (128, 128), 0) & 3
    shift = jnp.where(
        digit_of == 0, 12, jnp.where(digit_of == 1, 6, jnp.where(digit_of == 2, 0, 18))
    )
    positions = []
    for block in range(count // 128):
        at = slice(block * 128, (block + 1) * 128)
        part = labels[:, at]
        member = lax.broadcasted_iota(jnp.int32, (devices, 128), 0) == part
        ones = member.astype(jnp.float32).astype(jnp.bfloat16)
        members[:, at] = ones
        sums = jnp.dot(ones, before, preferred_element_type=jnp.float32)
        rank = jnp.where(member, sums[:, :128] + carry, 0.0)
        carry = carry + sums[:, 128:]
        position = jnp.sum(rank, axis=0, keepdims=True).astype(jnp.int32)
        positions.append(position)
        turned = (position + 2 * ((me - part) & 3)) & 7
        lane_ref[:, at] = jnp.where(position < MAIN, turned, MAIN + turned)
        digit = ((order_ref[:, at] + 262144) >> shift) & 63
        marks[:, at] = (
            jnp.where(slot_of == position, digit, 0).astype(jnp.float32).astype(jnp.bfloat16)
        )
    for copy in large:
        copy.wait()

    position = jnp.concatenate(positions, axis=1)
    index = lax.broadcasted_iota(jnp.int32, (128, 128), 0).astype(jnp.float32)
    index = jnp.concatenate([index.astype(jnp.bfloat16)] * (count // 128), axis=1)
    index = index.reshape(8, 16, count)
    one, zero = jnp.ones((), jnp.bfloat16), jnp.zeros((), jnp.bfloat16)

    def choose(pick, first, chosen, code):
        code = jnp.where(chosen, code, -1).astype(jnp.float32)
        code = jnp.broadcast_to(code, (16, count)).astype(jnp.bfloat16)
        pick[first : first + 128, :] = jnp.where(index == code[None], one, zero).reshape(
            128, count
        )

    for block in range(main_rows // 128):
        choose(
            pick,
            block * 128,
            ((labels >> 4) == block) & (position < MAIN),
            (labels & 15) * MAIN + position,
        )
    for block in range(tail_rows // 128):
        choose(
            tail_pick,
            block * 128,
            ((labels >> 5) == block) & (position >= MAIN),
            (labels & 31) * TAIL + position - MAIN,
        )
    places[...] = lax.dot_general(
        members[...], marks[...], NT, preferred_element_type=jnp.float32
    )

    for k in range(parts):
        at = slice(k * part_rows, (k + 1) * part_rows)
        values = rows[at, :].astype(jnp.float32)
        scale = lax.rsqrt(
            jnp.mean(values * values, axis=1, keepdims=True) + 1e-06
        ) * width ** (-0.5)
        values = (values * scale).astype(jnp.bfloat16)
        for n, columns in enumerate(unit):
            columns[at, :] = values[:, n * step : (n + 1) * step]

    turn = lax.broadcasted_iota(jnp.int32, (8, 128), 0) >> 1

    def put(tile, values):
        values = values.reshape(groups, GROUP, 8, 128)
        if tile:
            for e in range(GROUP):
                out_ref[:, CAP * e + tile] = values[:, e].astype(jnp.bfloat16)
            return
        for group in range(groups):
            out_ref[group, 0] = values[group, 0].astype(jnp.bfloat16)
            for e in range(1, GROUP + 1):
                at = group * GROUP + e - 1
                mixed = jnp.where(
                    turn == e - 1,
                    jnp.broadcast_to(places[at : at + 1, :], (8, 128)),
                    values[group, e - 1],
                )
                if e < GROUP:
                    mixed = jnp.where(turn >= e, values[group, e], mixed)
                out_ref[group, CAP * e] = mixed.astype(jnp.bfloat16)

    upper = lax.broadcasted_iota(jnp.int32, (devices // 2, 8, step), 1) >= 4
    for n in range(half // step):
        ends = (n * step, half + n * step)
        for first in ends:
            main = jnp.dot(
                pick[...],
                unit[first // step][...],
                preferred_element_type=jnp.float32,
            )
            for k in range(step // 128):
                put(first // 128 + k, main[:, k * 128 : (k + 1) * 128])
        low, high = (
            jnp.dot(
                tail_pick[...],
                unit[first // step][...],
                preferred_element_type=jnp.float32,
            ).reshape(devices // 2, 8, step)
            for first in ends
        )
        folded = jnp.stack(
            [
                jnp.where(upper, pltpu.roll(high, 4, 1), low),
                jnp.where(upper, high, pltpu.roll(low, 4, 1)),
            ],
            axis=1,
        ).reshape(devices, 8, step)
        for k in range(step // 128):
            put(MAIN + n * step // 128 + k, folded[:, :, k * 128 : (k + 1) * 128])


def score_kernel(
    got_ref, best_ref, digits, row_best, results, ordered, *blocks
):
    groups = got_ref.shape[0]
    devices = groups * GROUP
    member, column = blocks[: len(blocks) // 2], blocks[len(blocks) // 2 :]
    step, width = member[0].shape
    docs = step * len(member)
    pieces = width // 128
    main_rows = devices * MAIN
    last = GROUP * CAP
    me = lax.axis_index("blk")
    line = lax.broadcasted_iota(jnp.int32, (8, 128), 0)
    lane = lax.broadcasted_iota(jnp.int32, (8, 128), 1)
    turn, owner = line >> 1, lane >> 2
    inner = (turn == 1) | (turn == 2)
    first_half = turn < 2

    def both(a, b):
        return jnp.concatenate([a, b], axis=0).astype(jnp.bfloat16)

    def put(first, t, values):
        at = slice(first % step, first % step + 16)
        member[first // step][at, t * 128 : (t + 1) * 128] = values

    for group in range(groups):
        chunks = []
        for turns in range(GROUP):
            source = (me + turns) & 3
            base = CAP * source - jnp.where(source < me, 1, 0)
            tiles = [
                got_ref[group, jnp.clip(base + t, 0, last)].astype(jnp.float32)
                for t in range(CAP + 2)
            ]
            if turns:
                tiles = [
                    jnp.where(turn >= turns, tiles[t], tiles[t + 1]) for t in range(CAP + 1)
                ]
            tiles[0] = jnp.where(((turn - turns) & 3) >= me, tiles[0], tiles[CAP])
            chunks.append(tiles)
        places = got_ref[group, last].astype(jnp.float32)
        for e in range(GROUP - 1):
            places = jnp.where(
                turn == e, got_ref[group, CAP * (e + 1)].astype(jnp.float32), places
            )
        places = pltpu.roll(places, (8 - 2 * me) & 7, 0)
        places = [
            jnp.broadcast_to(places[2 * turns : 2 * turns + 1, :], (8, 128))
            for turns in range(GROUP)
        ]
        for k in range(2):
            a, b = TURNS[2 * k], TURNS[2 * k + 1]
            at = slice(group * 32 + k * 16, group * 32 + k * 16 + 16)
            for t in range(pieces):
                put(at.start, t, both(chunks[a][t], chunks[b][t]))
            digits[at, :] = both(
                *(
                    jnp.where(owner == ((line - 2 * turns) & 7), places[turns], 0.0)
                    for turns in (a, b)
                )
            )
        at = slice(main_rows + group * 16, main_rows + group * 16 + 16)
        for t in range(pieces // 2):
            a, b, c, d = (chunks[turns][MAIN + t] for turns in range(GROUP))
            put(at.start, t, both(jnp.where(first_half, a, c), jnp.where(inner, b, d)))
            t = t + pieces // 2
            high = both(
                pltpu.roll(jnp.where(first_half, c, a), 4, 0),
                pltpu.roll(jnp.where(inner, d, b), 4, 0),
            )
            put(at.start, t, high)
        digits[at, :] = both(
            jnp.where(
                owner == MAIN + (line & 3), jnp.where(first_half, places[0], places[2]), 0.0
            ),
            jnp.where(
                owner == MAIN + ((line - 2) & 3), jnp.where(inner, places[1], places[3]), 0.0
            ),
        )

    def weights(shape, axis):
        at = lax.broadcasted_iota(jnp.int32, shape, axis)
        digit = at & 3
        weight = jnp.where(
            digit == 0,
            4096.0,
            jnp.where(digit == 1, 64.0, jnp.where(digit == 2, 1.0, -262144.0)),
        )
        return jnp.where(at < 4 * CAP, weight, 0.0).astype(jnp.bfloat16)

    for i, places in enumerate(column):
        places[...] = jnp.dot(
            digits[i * step : (i + 1) * step, :],
            weights((128, 128), 0),
            preferred_element_type=jnp.float32,
        )
    place_row = lax.dot_general(
        weights((8, 128), 1), digits[...], NT, preferred_element_type=jnp.float32
    )
    col_best = [jnp.full((8, 128), -1.0, jnp.float32)] * (docs // 128)
    for i in range(docs // step):
        best = jnp.full((step, 128), -1.0, jnp.float32)
        for j in range(i + 1):
            scores = lax.dot_general(
                member[i][...], member[j][...], NT, preferred_element_type=jnp.float32
            )
            for k in range(step // 128):
                at = j * step + k * 128
                part = scores[:, k * 128 : (k + 1) * 128]
                earlier = place_row[0:1, at : at + 128] < column[i][...]
                best = jnp.maximum(best, jnp.where(earlier, part, -1.0))
                if j != i:
                    other = jnp.where(earlier, -1.0, part)
                    col_best[at // 128] = jnp.maximum(
                        col_best[at // 128],
                        jnp.max(other.reshape(step // 8, 8, 128), axis=0),
                    )
        best = jnp.broadcast_to(jnp.max(best, axis=1, keepdims=True), (step, 128))
        place = lax.broadcasted_iota(jnp.int32, (step, 128), 0) & 7
        if i * step >= main_rows:
            place = place + MAIN
        best = jnp.where(lax.broadcasted_iota(jnp.int32, (step, 128), 1) == place, best, -2.0)
        row_best[i * step // 8 : (i + 1) * step // 8, :] = jnp.max(
            best.reshape(step // 8, 8, 128), axis=1
        )

    own = (
        lax.broadcasted_iota(jnp.int32, (16, 128), 1) >> 3
        == lax.broadcasted_iota(jnp.int32, (16, 128), 0)
    )
    for block in range(docs // 128):
        best = jnp.max(col_best[block], axis=0, keepdims=True)
        best = jnp.where(own, jnp.broadcast_to(best, (16, 128)), -2.0)
        for shift in (64, 32, 16, 8):
            best = jnp.maximum(best, pltpu.roll(best, shift, 1))
        at = slice(block * 16, (block + 1) * 16)
        results[at, :] = jnp.maximum(best, row_best[at, :])
    lane = lax.broadcasted_iota(jnp.int32, (groups, 128), 1)
    for index, turns in enumerate(TURNS):
        best = jnp.where(
            lane < MAIN,
            results[pl.ds(index, groups, stride=GROUP), :],
            results[pl.ds(devices + index // 2, groups, stride=2), :],
        )
        for e in range(GROUP):

            @pl.when(me == e)
            def _():
                ordered[pl.ds((e + turns) % GROUP, groups, stride=GROUP), :] = best

    best_ref[...] = ordered[:devices, :]


def pick_kernel(got_ref, label_ref, lane_ref, out_ref):
    devices = got_ref.shape[0]
    count = label_ref.shape[1]
    table = got_ref[...].T[: 2 * MAIN, :]
    top = table.astype(jnp.bfloat16).astype(jnp.float32)
    rest = table - top
    middle = rest.astype(jnp.bfloat16).astype(jnp.float32)
    parts = jnp.concatenate([top, middle, rest - middle], axis=0).astype(jnp.bfloat16)
    chosen = lax.broadcasted_iota(jnp.int32, (devices, count), 0) == label_ref[...]
    values = jnp.dot(
        parts,
        chosen.astype(jnp.float32).astype(jnp.bfloat16),
        preferred_element_type=jnp.float32,
    )
    values = (values[: 2 * MAIN] + values[2 * MAIN : 4 * MAIN]) + values[4 * MAIN :]
    line = lax.broadcasted_iota(jnp.int32, (2 * MAIN, count), 0)
    out_ref[...] = jnp.sum(
        jnp.where(line == lane_ref[...], values, 0.0), axis=0, keepdims=True
    )


def shards(embeddings, labels, order_ids):
    rows, width = embeddings.shape
    devices = lax.axis_size("grp") * lax.axis_size("blk")
    groups, units = devices // GROUP, GROUP * CAP + 1
    docs, step = devices * CAP, 256
    params = pltpu.CompilerParams(vmem_limit_bytes=VMEM_LIMIT)
    in_hbm = pl.BlockSpec(memory_space=pltpu.HBM)
    outgoing, lane_row, label_row = pl.pallas_call(
        place_kernel,
        in_specs=[in_hbm] * 3,
        out_shape=[
            jax.ShapeDtypeStruct((groups, units, 8, 128), jnp.bfloat16),
            jax.ShapeDtypeStruct((1, rows), jnp.int32),
            jax.ShapeDtypeStruct((1, rows), jnp.int32),
        ],
        scratch_shapes=[
            pltpu.VMEM((rows, width), jnp.bfloat16),
            pltpu.VMEM((1, rows), jnp.int32),
            pltpu.VMEM((devices * MAIN, rows), jnp.bfloat16),
            pltpu.VMEM((devices * TAIL, rows), jnp.bfloat16),
            pltpu.VMEM((devices, rows), jnp.bfloat16),
            pltpu.VMEM((128, rows), jnp.bfloat16),
            pltpu.VMEM((devices, 128), jnp.float32),
            pltpu.SemaphoreType.DMA((6,)),
        ]
        + [pltpu.VMEM((rows, step), jnp.bfloat16)] * (width // step),
        compiler_params=params,
        name="place",
    )(
        *(
            pltpu.with_memory_space_constraint(x, pltpu.HBM)
            for x in (embeddings, labels.reshape(1, rows), order_ids.reshape(1, rows))
        )
    )
    got = lax.all_to_all(
        outgoing.reshape(devices, units, 2, 128),
        ("grp", "blk"),
        split_axis=0,
        concat_axis=0,
        tiled=True,
    )
    best = pl.pallas_call(
        score_kernel,
        out_shape=jax.ShapeDtypeStruct((devices, 128), jnp.float32),
        scratch_shapes=[
            pltpu.VMEM((docs, 128), jnp.bfloat16),
            pltpu.VMEM((docs // 8, 128), jnp.float32),
            pltpu.VMEM((docs // 8 + 8, 128), jnp.float32),
            pltpu.VMEM((devices + 8, 128), jnp.float32),
        ]
        + [pltpu.VMEM((step, width), jnp.bfloat16)] * (docs // step)
        + [pltpu.VMEM((step, 128), jnp.float32)] * (docs // step),
        compiler_params=params,
        name="score",
    )(got.reshape(groups, units, 8, 128))
    returned = lax.all_to_all(
        best.reshape(devices, 1, 128), ("grp", "blk"), split_axis=0, concat_axis=0, tiled=True
    ).reshape(devices, 128)
    picked = pl.pallas_call(
        pick_kernel,
        out_shape=jax.ShapeDtypeStruct((1, rows), jnp.float32),
        compiler_params=params,
        name="pick",
    )(returned, label_row, lane_row)
    return picked.reshape(rows)


def solution(mesh):
    placed = (P(("grp", "blk"), None), P(("grp", "blk"), None), P(("grp", "blk")))
    return jax.shard_map(
        shards, mesh=mesh, in_specs=placed, out_specs=P(("grp", "blk")), check_vma=False
    )
```
